32 devices in a mesh: expert: 16 (over z, y, x), hidden: 2 (over core).
Axes of the slice: x: 2, y: 2, z: 4, core: 2. Of those that a mesh axis runs over, the one named last changes fastest.
Arguments:
- tokens: bfloat16 [2, 32, 2048], P('hidden', 'expert'), may hold values from -6 to 6
- grad_out: bfloat16 [2, 32, 2048], P('hidden', 'expert'), may hold values from -6 to 6
- expert_ids: int32 [2, 32, 8], P('hidden', 'expert'), may hold values from 0 to 15, all different within a row; in each aligned block of 32 rows (0 to 31, 32 to 63, ..., all dimensions but the last counted through in order) at most 32 rows name the same one
- router_logits: float32 [2, 32, 8], P('hidden', 'expert'), may hold values from -4 to 4
- w_gate: bfloat16 [16, 2048, 1536], P('expert', None, 'hidden'), may hold values from -0.125 to 0.125
- w_up: bfloat16 [16, 2048, 1536], P('expert', None, 'hidden'), may hold values from -0.125 to 0.125
- w_down: bfloat16 [16, 1536, 2048], P('expert', 'hidden'), may hold values from -0.15625 to 0.15625
Outputs:
- grad_in: float32 [2, 32, 2048], P('hidden', 'expert')
- grad_logits: float32 [2, 32, 8], P('hidden', 'expert')
- grad_gate: float32 [16, 2048, 1536], P('expert', None, 'hidden')
- grad_up: float32 [16, 2048, 1536], P('expert', None, 'hidden')
- grad_down: float32 [16, 1536, 2048], P('expert', 'hidden')
The draws below stay inside these ranges and needn't reach their ends.
Inputs may be any that keep to these rules, and one draw needn't show every extreme that they name: `expert_ids`: each token names 8 different experts. Among the tokens of one hidden index no expert is named more than 32 times, a bound that some block reaches.
All inputs are finite; a program needn't handle non-finite values.
Results may differ from the reference program's by a relative error of at most 0.0041.
Values may be sent and summed in bfloat16 or wider, within the bound.
No kernel may reach another device: no remote copies, remote signals or barrier semaphores. Data moves between devices by JAX's collectives and lax.ppermute only.
A program may use at most 64 MiB of HBM per device.

```python
import math
import jax
import jax.numpy as jnp
import numpy as np
from jax import lax

D = 2048
FF = 1536
TOP = 8
EXPERTS = 16
TOK_SL = 32
CAP = 32
N_HIDDEN = 2


def levels(key, dims, shards, smallest, top_value):
    gain, own = 1.0, jax.random.fold_in(key, 6)
    for axis_at, parts in shards:
        heights = jnp.exp(jax.random.uniform(jax.random.fold_in(own, axis_at), (parts,), jnp.float32, smallest / len(shards), top_value / len(shards)))
        gain = gain * jnp.repeat(heights, dims[axis_at] // parts).reshape([-1 if axis == axis_at else 1 for axis in range(len(dims))])
    return gain


def assign_block(key, own, number, rows, count, top, most, skew):
    order = jax.random.permutation(key, count)
    packed, usual = portions_of(count, rows * top, most, skew, True), portions_of(count, rows * top, most, skew, False)
    places = jnp.arange(count)

    def named(lengths, offset_by):
        used = int((lengths > 0).sum())
        fixed = max(1, used // 4)
        passed = fixed + (places - fixed + offset_by * (used - fixed)) % max(1, count - fixed)
        return jnp.zeros((count,), jnp.int32).at[order[jnp.where(places < fixed, places, passed)]].set(jnp.asarray(lengths, jnp.int32))

    lengths = jnp.where(number % 4 == 0, named(packed, number // 4), named(usual, number - number // 4 - 1))
    mixed = jax.random.permutation(jax.random.fold_in(own, 3), count)
    donor, taker = mixed[0:count // 2 * 2:2], mixed[1:count // 2 * 2:2]
    margin = jnp.minimum(lengths[donor] - 1, most - lengths[taker]) // 2
    margin = jnp.where((donor == order[0]) | (taker == order[0]) | (lengths[taker] == 0), 0, jnp.maximum(margin, 0))
    passed = jax.random.randint(jax.random.fold_in(own, 4), (count // 2,), 0, 1 << 20) % (margin + 1)
    lengths = lengths.at[donor].add(-passed).at[taker].add(passed)
    labels = jnp.searchsorted(jnp.cumsum(lengths), jnp.arange(rows * top), side="right").astype(jnp.int32)
    table = labels.reshape(top, rows).T
    table = table[jax.random.permutation(jax.random.fold_in(own, 1), rows)]
    offset_by = jax.random.randint(jax.random.fold_in(own, 2), (rows, 1), 0, top)
    return jnp.take_along_axis(table, (jnp.arange(top)[None, :] + offset_by) % top, axis=1)


def portions_of(count, total, limit, skew, full):
    loads = [(1 << 20) // math.isqrt(standing ** skew) + 1 for standing in range(1, count + 1)]
    largest = limit if full else min(limit, max(-(-total // count), total * loads[0] // sum(loads)))
    least = 1 if total - largest >= count - 1 else 0
    given, surplus = [largest] + [least] * (count - 1), total - largest - least * (count - 1)
    while surplus > 0:
        movable = [i for i in range(1, count) if given[i] < largest] or [i for i in range(1, count) if given[i] < limit]
        pool, remaining = sum([loads[i] for i in movable]), surplus
        for i in movable:
            more = min(limit - given[i], max(1, remaining * loads[i] // pool), surplus)
            given[i] = given[i] + more
            surplus = surplus - more
    return np.array(given)


def noise(key, shape, deviation, most, pieces=(), kind=jnp.bfloat16):
    entries = deviation * jax.random.normal(key, shape, jnp.float32)
    if pieces:
        entries = entries * levels(key, shape, pieces, -0.22, 0.18)
    return jnp.clip(entries, -most, most).astype(kind)


def setup_inputs(seed: int = 0) -> dict:
    key_of = jax.random.split(jax.random.key(seed), 8)
    tokens = noise(key_of[0], (N_HIDDEN, TOK_SL, D), 1.0, 6.0, ((0, 2), (1, 16)))
    grad_out = noise(key_of[1], (N_HIDDEN, TOK_SL, D), 1.0, 6.0, ((0, 2), (1, 16)))
    expert_ids_keys = jax.random.split(jax.random.fold_in(key_of[2], 1), N_HIDDEN * TOK_SL // TOK_SL)
    expert_ids_turns = jax.random.permutation(jax.random.fold_in(key_of[2], 3), N_HIDDEN * TOK_SL // TOK_SL)
    expert_ids = jax.vmap(lambda own, number: assign_block(jax.random.fold_in(key_of[2], 2), own, number, TOK_SL, EXPERTS, TOP, CAP, 2))(expert_ids_keys, expert_ids_turns).reshape((N_HIDDEN, TOK_SL, TOP))
    router_logits = noise(key_of[3], (N_HIDDEN, TOK_SL, TOP), 1.0, 4.0, ((0, 2), (1, 16)), jnp.float32)
    w_gate = noise(key_of[4], (EXPERTS, D, FF), D ** -0.5, 0.125, ((0, 16), (2, 2)))
    w_up = noise(key_of[5], (EXPERTS, D, FF), D ** -0.5, 0.125, ((0, 16), (2, 2)))
    w_down = noise(key_of[6], (EXPERTS, FF, D), FF ** -0.5, 0.15625, ((0, 16), (1, 2)))
    return {"tokens": tokens, "grad_out": grad_out, "expert_ids": expert_ids, "router_logits": router_logits, "w_gate": w_gate, "w_up": w_up, "w_down": w_down}


def expert_grads(x_rows, grad_rows, gate_col, gate_weight, up_weight, down_weight):
    pre_gate = jnp.dot(x_rows, gate_weight, preferred_element_type=jnp.float32)
    pre_up = jnp.dot(x_rows, up_weight, preferred_element_type=jnp.float32)
    back_grad = lax.dot_general(grad_rows, down_weight, (((1,), (1,)), ((), ())), preferred_element_type=jnp.float32)
    sigmoid_gate = jax.nn.sigmoid(pre_gate)
    silu_gate = pre_gate * sigmoid_gate
    active = silu_gate * pre_up
    gate_grad = jnp.sum(active * back_grad, axis=-1)
    weight = gate_col.astype(jnp.float32)
    scaled = (weight * active).astype(jnp.bfloat16)
    weighted_back = weight * back_grad
    d_gate_pre = (weighted_back * pre_up * sigmoid_gate * (1.0 + pre_gate * (1.0 - sigmoid_gate))).astype(jnp.bfloat16)
    d_up_pre = (weighted_back * silu_gate).astype(jnp.bfloat16)
    row_grad = lax.dot_general(d_gate_pre, gate_weight, (((1,), (1,)), ((), ())), preferred_element_type=jnp.float32)
    row_grad = row_grad + lax.dot_general(d_up_pre, up_weight, (((1,), (1,)), ((), ())), preferred_element_type=jnp.float32)
    sum_gate = lax.dot_general(x_rows, d_gate_pre, (((0,), (0,)), ((), ())), preferred_element_type=jnp.float32)
    sum_up = lax.dot_general(x_rows, d_up_pre, (((0,), (0,)), ((), ())), preferred_element_type=jnp.float32)
    sum_down = lax.dot_general(scaled, grad_rows, (((0,), (0,)), ((), ())), preferred_element_type=jnp.float32)
    return row_grad, gate_grad, sum_gate, sum_up, sum_down


def reference(tokens, grad_out, expert_ids, router_logits, w_gate, w_up, w_down):
    highest = lax.Precision.HIGHEST
    raised = jnp.exp(router_logits)
    gate_probs = raised / jnp.sum(raised, axis=-1, keepdims=True)
    gate_rows = gate_probs.astype(jnp.bfloat16)
    tokens_wide = tokens.astype(jnp.float32)
    grads_wide = grad_out.astype(jnp.float32)
    positions = jnp.arange(CAP, dtype=jnp.int32)

    def per_expert(totals, expert):
        input_acc, logit_acc = totals
        chosen = expert_ids == expert
        column = jnp.sum(jnp.where(chosen, gate_rows.astype(jnp.float32), jnp.float32(0.0)), axis=-1)
        picked = jnp.any(chosen, axis=-1)
        row_order = jnp.cumsum(picked.astype(jnp.int32), axis=1) - 1
        placing = ((row_order[:, None, :] == positions[None, :, None]) & picked[:, None, :]).astype(jnp.float32)
        x_rows = jnp.einsum("hct,htd->hcd", placing, tokens_wide, precision=highest).astype(jnp.bfloat16).reshape(N_HIDDEN * CAP, D)
        grad_rows = jnp.einsum("hct,htd->hcd", placing, grads_wide, precision=highest).astype(jnp.bfloat16).reshape(N_HIDDEN * CAP, D)
        gate_col = jnp.einsum("hct,ht->hc", placing, column, precision=highest).reshape(N_HIDDEN * CAP, 1)
        gate_weight = lax.dynamic_index_in_dim(w_gate, expert, 0, keepdims=False)
        up_weight = lax.dynamic_index_in_dim(w_up, expert, 0, keepdims=False)
        down_weight = lax.dynamic_index_in_dim(w_down, expert, 0, keepdims=False)
        row_grad, gate_grad, sum_gate, sum_up, sum_down = expert_grads(x_rows, grad_rows, gate_col, gate_weight, up_weight, down_weight)
        input_acc = input_acc + jnp.einsum("hct,hcd->htd", placing, row_grad.reshape(N_HIDDEN, CAP, D), precision=highest)
        token_gate = jnp.einsum("hct,hc->ht", placing, gate_grad.reshape(N_HIDDEN, CAP), precision=highest)
        logit_acc = logit_acc + jnp.where(chosen, token_gate[:, :, None], jnp.float32(0.0))
        return (input_acc, logit_acc), (sum_gate, sum_up, sum_down)

    start_state = (jnp.zeros((N_HIDDEN, TOK_SL, D), jnp.float32), jnp.zeros((N_HIDDEN, TOK_SL, TOP), jnp.float32))
    finals, stacked = lax.scan(per_expert, start_state, jnp.arange(EXPERTS, dtype=jnp.int32))
    input_acc, gate_grad = finals
    grad_logits = gate_probs * (gate_grad - jnp.sum(gate_probs * gate_grad, axis=-1, keepdims=True))
    return input_acc, grad_logits, stacked[0], stacked[1], stacked[2]
```

```python
import functools

import jax
import jax.numpy as jnp
from jax import lax
from jax.experimental import pallas as pl
from jax.experimental.pallas import tpu as pltpu
from jax.sharding import PartitionSpec as P

TOP = 8
LANES = 128
VMEM_A = 24 * 2**20
VMEM_B = 16 * 2**20
BAND = 256


def expert_core(x_rows, grad_rows, gate_col, gate_weight, up_weight, down_weight):
    pre_gate = jnp.dot(x_rows, gate_weight, preferred_element_type=jnp.float32)
    pre_up = jnp.dot(x_rows, up_weight, preferred_element_type=jnp.float32)
    back_grad = lax.dot_general(
        grad_rows, down_weight, (((1,), (1,)), ((), ())), preferred_element_type=jnp.float32
    )
    sigmoid_gate = jax.nn.sigmoid(pre_gate)
    silu_gate = pre_gate * sigmoid_gate
    active = silu_gate * pre_up
    gate_grad = jnp.sum(active * back_grad, axis=-1)
    weight = gate_col.astype(jnp.float32)
    scaled = (weight * active).astype(jnp.bfloat16)
    weighted_back = weight * back_grad
    d_gate_pre = (
        weighted_back * pre_up * sigmoid_gate * (1.0 + pre_gate * (1.0 - sigmoid_gate))
    ).astype(jnp.bfloat16)
    d_up_pre = (weighted_back * silu_gate).astype(jnp.bfloat16)
    sum_gate = lax.dot_general(
        x_rows, d_gate_pre, (((0,), (0,)), ((), ())), preferred_element_type=jnp.float32
    )
    sum_up = lax.dot_general(
        x_rows, d_up_pre, (((0,), (0,)), ((), ())), preferred_element_type=jnp.float32
    )
    sum_down = lax.dot_general(
        scaled, grad_rows, (((0,), (0,)), ((), ())), preferred_element_type=jnp.float32
    )
    return (gate_grad, d_gate_pre, d_up_pre, sum_gate, sum_up, sum_down)


def project_back(d_gate_pre, d_up_pre, gate_weight, up_weight):
    row_grad = lax.dot_general(
        d_gate_pre, gate_weight, (((1,), (1,)), ((), ())), preferred_element_type=jnp.float32
    )
    return row_grad + lax.dot_general(
        d_up_pre, up_weight, (((1,), (1,)), ((), ())), preferred_element_type=jnp.float32
    )


def routed_rows(tokens, grad_out, expert_ids, router_logits, w_gate, w_up, w_down):
    highest = lax.Precision.HIGHEST
    tok_dev = tokens.shape[1]
    peers = lax.axis_size("expert")
    mine = lax.axis_index("expert")
    row_cap = min(2 * tok_dev * TOP, tok_dev * peers)
    raised = jnp.exp(router_logits[0])
    gate_probs = raised / jnp.sum(raised, axis=-1, keepdims=True)
    gate_rows = gate_probs.astype(jnp.bfloat16)
    expert_range = jnp.arange(peers, dtype=jnp.int32)
    chosen = expert_ids[0][:, :, None] == expert_range[None, None, :]
    per_peer = jnp.sum(
        jnp.where(chosen, gate_rows.astype(jnp.float32)[:, :, None], jnp.float32(0.0)), axis=1
    )
    gate_table = per_peer.astype(jnp.bfloat16)
    got_x, got_grad, got_table = (
        lax.all_gather(tokens, "expert", axis=1, tiled=True),
        lax.all_gather(grad_out, "expert", axis=1, tiled=True),
        lax.all_gather(gate_table[None], "expert", axis=1, tiled=True),
    )
    all_x = got_x[0]
    all_grad = got_grad[0]
    column = jnp.sum(
        jnp.where(
            expert_range[None, :] == mine, got_table[0].astype(jnp.float32), jnp.float32(0.0)
        ),
        axis=-1,
    )
    picked = column > 0.0
    row_order = jnp.cumsum(picked.astype(jnp.int32)) - 1
    placing = (row_order[None, :] == jnp.arange(row_cap, dtype=jnp.int32)[:, None]) & picked[
        None, :
    ]
    placing_half = placing.astype(jnp.bfloat16)
    placing_full = placing.astype(jnp.float32)
    x_rows = jnp.dot(placing_half, all_x, preferred_element_type=jnp.float32).astype(jnp.bfloat16)
    grad_rows = jnp.dot(placing_half, all_grad, preferred_element_type=jnp.float32).astype(
        jnp.bfloat16
    )
    gate_col = jnp.dot(placing_full, column, precision=highest).astype(jnp.bfloat16)[:, None]
    gate_weight = w_gate[0]
    up_weight = w_up[0]
    down_weight = w_down[0]
    cycle_x, cycle_grad, cycle_gate = (
        lax.all_gather(x_rows, "hidden", axis=0, tiled=True),
        lax.all_gather(grad_rows, "hidden", axis=0, tiled=True),
        lax.all_gather(gate_col, "hidden", axis=0, tiled=True),
    )
    gate_part, gate_pre_all, up_pre_all, sum_gate, sum_up, sum_down = expert_core(
        cycle_x, cycle_grad, cycle_gate, gate_weight, up_weight, down_weight
    )
    row_part = project_back(gate_pre_all, up_pre_all, gate_weight, up_weight)
    own_rows, own_gate = (
        lax.psum_scatter(row_part, "hidden", scatter_dimension=0, tiled=True),
        lax.psum_scatter(gate_part, "hidden", scatter_dimension=0, tiled=True),
    )
    dense = lax.dot_general(placing_full, own_rows, (((0,), (0,)), ((), ())), precision=highest)
    token_gate = lax.dot_general(
        placing_full, own_gate, (((0,), (0,)), ((), ())), precision=highest
    )
    gate_out = jnp.where(expert_range[None, :] == mine, token_gate[:, None], jnp.float32(0.0))
    summed, gate_sums = (
        lax.psum_scatter(dense[None], "expert", scatter_dimension=1, tiled=True),
        lax.psum_scatter(gate_out[None], "expert", scatter_dimension=1, tiled=True),
    )
    gate_grad = jnp.sum(jnp.where(chosen, gate_sums[0][:, None, :], jnp.float32(0.0)), axis=-1)
    grad_logits = gate_probs * (gate_grad - jnp.sum(gate_probs * gate_grad, axis=-1, keepdims=True))
    return (summed, grad_logits[None], sum_gate[None], sum_up[None], sum_down[None])


def gate_probs_of(logits):
    raised = jnp.exp(logits)
    return raised / jnp.sum(raised, axis=-1, keepdims=True)


def pack_kernel(tokens_ref, grads_ref, ids_ref, logits_ref, out_ref):
    peers, tok_dev, _ = out_ref.shape
    depth = tokens_ref.shape[-1]
    gates = gate_probs_of(logits_ref[0]).astype(jnp.bfloat16).astype(jnp.float32)
    ids = ids_ref[0]
    wide = (tok_dev, LANES)
    named = [jnp.broadcast_to(ids[:, k : k + 1], wide) for k in range(TOP)]
    shares = [jnp.broadcast_to(gates[:, k : k + 1], wide) for k in range(TOP)]
    tokens, grads = tokens_ref[0], grads_ref[0]
    for peer in range(peers):
        gate = jnp.zeros(wide, jnp.float32)
        for k in range(TOP):
            gate = jnp.where(named[k] == peer, shares[k], gate)
        out_ref[peer, :, :depth] = tokens
        out_ref[peer, :, depth : 2 * depth] = grads
        out_ref[peer, :, 2 * depth :] = gate.astype(jnp.bfloat16)


def rows_kernel(n_parts, place_ref, *refs):
    parts = refs[:n_parts]
    w_gate_ref, w_up_ref, w_down_ref = refs[n_parts : n_parts + 3]
    send_ref, x_ref, o_ref, scaled_ref, d_gate_ref, d_up_ref, out_rows = refs[n_parts + 3 :]
    peers, tok_dev, _ = parts[0].shape
    depth = x_ref.shape[1]
    gate_cols = []
    for s, part in enumerate(parts):
        for peer in range(peers):
            at = (s * peers + peer) * tok_dev
            x_ref[at : at + tok_dev, :] = part[peer, :, :depth]
            o_ref[at : at + tok_dev, :] = part[peer, :, depth : 2 * depth]
            out_rows[at : at + tok_dev, depth : depth + LANES] = part[peer, :, 2 * depth :].astype(
                jnp.float32
            )
    weight = out_rows[:, depth : depth + 1]
    x_rows, grad_rows = x_ref[...], o_ref[...]
    pre_gate = jnp.dot(x_rows, w_gate_ref[0], preferred_element_type=jnp.float32)
    pre_up = jnp.dot(x_rows, w_up_ref[0], preferred_element_type=jnp.float32)
    across = (((1,), (1,)), ((), ()))
    back_grad = lax.dot_general(
        grad_rows, w_down_ref[0], across, preferred_element_type=jnp.float32
    )
    sigmoid_gate = 1.0 / (1.0 + jnp.exp(-pre_gate))
    silu_gate = pre_gate * sigmoid_gate
    active = silu_gate * pre_up
    gate_part = jnp.sum(active * back_grad, axis=-1, keepdims=True)
    weighted_back = weight * back_grad
    d_gate = (
        weighted_back * pre_up * sigmoid_gate * (1.0 + pre_gate * (1.0 - sigmoid_gate))
    ).astype(jnp.bfloat16)
    d_up = (weighted_back * silu_gate).astype(jnp.bfloat16)
    scaled_ref[...] = (weight * active).astype(jnp.bfloat16)
    d_gate_ref[...] = d_gate
    d_up_ref[...] = d_up
    out_rows[:, :depth] = lax.dot_general(
        d_gate, w_gate_ref[0], across, preferred_element_type=jnp.float32
    ) + lax.dot_general(d_up, w_up_ref[0], across, preferred_element_type=jnp.float32)
    mine, here = place_ref[0], place_ref[1]
    rows = out_rows.shape[0]
    lane = lax.broadcasted_iota(jnp.int32, (rows, LANES), 1)
    high = gate_part.astype(jnp.bfloat16).astype(jnp.float32)
    out_rows[:, depth : depth + LANES] = jnp.where(lane == mine, high, 0.0)
    out_rows[:, depth + LANES :] = jnp.where(lane == mine, gate_part - high, 0.0)
    for s in range(n_parts):
        owner = lax.rem(here + n_parts - s, n_parts)
        for peer in range(peers):
            at = (s * peers + peer) * tok_dev
            send_ref[peer * n_parts + owner] = out_rows[at : at + tok_dev, :].astype(jnp.bfloat16)


def outer_kernel(x_ref, o_ref, scaled_ref, d_gate_ref, d_up_ref, gate_ref, up_ref, down_ref):
    over_rows = (((0,), (0,)), ((), ()))
    x_rows = x_ref[...]
    gate_ref[0] = lax.dot_general(
        x_rows, d_gate_ref[...], over_rows, preferred_element_type=jnp.float32
    )
    up_ref[0] = lax.dot_general(
        x_rows, d_up_ref[...], over_rows, preferred_element_type=jnp.float32
    )
    down_ref[0] = lax.dot_general(
        scaled_ref[...], o_ref[...], over_rows, preferred_element_type=jnp.float32
    )


def finish_kernel(got_ref, ids_ref, logits_ref, grad_in_ref, grad_logits_ref):
    depth = grad_in_ref.shape[-1]
    tok_dev = grad_in_ref.shape[1]
    total = got_ref[0].astype(jnp.float32)
    for block in range(1, got_ref.shape[0]):
        total = total + got_ref[block].astype(jnp.float32)
    grad_in_ref[0] = total[:, :depth]
    by_expert = total[:, depth : depth + LANES] + total[:, depth + LANES :]
    lane = lax.broadcasted_iota(jnp.int32, (tok_dev, LANES), 1)
    slot = lax.broadcasted_iota(jnp.int32, (tok_dev, TOP), 1)
    ids = ids_ref[0]
    gate_grad = jnp.zeros((tok_dev, TOP), jnp.float32)
    for k in range(TOP):
        hit = jnp.where(lane == ids[:, k : k + 1], by_expert, 0.0)
        gate_grad = jnp.where(slot == k, jnp.sum(hit, axis=-1, keepdims=True), gate_grad)
    probs = gate_probs_of(logits_ref[0])
    grad_logits_ref[0] = probs * (
        gate_grad - jnp.sum(probs * gate_grad, axis=-1, keepdims=True)
    )


def every_token(tokens, grad_out, expert_ids, router_logits, w_gate, w_up, w_down):
    peers, n_parts = lax.axis_size("expert"), lax.axis_size("hidden")
    tok_dev, depth = tokens.shape[1:]
    units = w_gate.shape[2]
    rows = n_parts * peers * tok_dev
    half = jnp.bfloat16
    shape = jax.ShapeDtypeStruct
    packed = pl.pallas_call(
        pack_kernel, out_shape=shape((peers, tok_dev, 2 * depth + LANES), half), name="pack"
    )(tokens, grad_out, expert_ids, router_logits)
    parts = [lax.all_to_all(packed, "expert", 0, 0, tiled=True)]
    for s in range(1, n_parts):
        turn = [(i, (i + s) % n_parts) for i in range(n_parts)]
        parts.append(lax.ppermute(parts[0], "hidden", turn))
    place = jnp.stack([lax.axis_index("expert"), lax.axis_index("hidden")]).astype(jnp.int32)
    in_vmem = pl.BlockSpec(memory_space=pltpu.VMEM)
    products = 2 * rows * depth * units
    send, x_rows, grad_rows, scaled, d_gate, d_up = pl.pallas_call(
        functools.partial(rows_kernel, n_parts),
        in_specs=[pl.BlockSpec(memory_space=pltpu.SMEM)] + [in_vmem] * (n_parts + 3),
        out_specs=[in_vmem] * 6,
        out_shape=[
            shape((peers * n_parts, tok_dev, depth + 2 * LANES), half),
            shape((rows, depth), half),
            shape((rows, depth), half),
            shape((rows, units), half),
            shape((rows, units), half),
            shape((rows, units), half),
        ],
        scratch_shapes=[pltpu.VMEM((rows, depth + 2 * LANES), jnp.float32)],
        compiler_params=pltpu.CompilerParams(vmem_limit_bytes=VMEM_A),
        cost_estimate=pl.CostEstimate(
            flops=5 * products, bytes_accessed=6 * depth * units, transcendentals=rows * units
        ),
        name="rows",
    )(place, *parts, w_gate, w_up, w_down)
    got = lax.all_to_all(send, ("expert", "hidden"), 0, 0, tiled=True)
    deep = min(BAND, depth)
    grad_gate, grad_up, grad_down = pl.pallas_call(
        outer_kernel,
        grid=(depth // deep,),
        in_specs=[
            pl.BlockSpec((rows, deep), lambda i: (0, i)),
            pl.BlockSpec((rows, deep), lambda i: (0, i)),
            pl.BlockSpec((rows, units), lambda i: (0, 0)),
            pl.BlockSpec((rows, units), lambda i: (0, 0)),
            pl.BlockSpec((rows, units), lambda i: (0, 0)),
        ],
        out_specs=[
            pl.BlockSpec((1, deep, units), lambda i: (0, i, 0)),
            pl.BlockSpec((1, deep, units), lambda i: (0, i, 0)),
            pl.BlockSpec((1, units, deep), lambda i: (0, 0, i)),
        ],
        out_shape=[
            shape((1, depth, units), jnp.float32),
            shape((1, depth, units), jnp.float32),
            shape((1, units, depth), jnp.float32),
        ],
        compiler_params=pltpu.CompilerParams(vmem_limit_bytes=VMEM_B),
        cost_estimate=pl.CostEstimate(
            flops=3 * products, bytes_accessed=12 * depth * units, transcendentals=0
        ),
        name="outer",
    )(x_rows, grad_rows, scaled, d_gate, d_up)
    grad_in, grad_logits = pl.pallas_call(
        finish_kernel,
        out_shape=[
            shape((1, tok_dev, depth), jnp.float32),
            shape((1, tok_dev, TOP), jnp.float32),
        ],
        name="finish",
    )(got, expert_ids, router_logits)
    return grad_in, grad_logits, grad_gate, grad_up, grad_down


def on_device(tokens, grad_out, expert_ids, router_logits, w_gate, w_up, w_down):
    tok_dev, peers = tokens.shape[1], lax.axis_size("expert")
    most, there = 2 * tok_dev * TOP, tok_dev * peers
    whole_lanes = tokens.shape[2] % BAND == 0 and w_gate.shape[2] % LANES == 0
    plan = every_token if there <= most and peers <= LANES and whole_lanes else routed_rows
    return plan(tokens, grad_out, expert_ids, router_logits, w_gate, w_up, w_down)


def solution(mesh):
    in_specs = (
        P("hidden", "expert", None),
        P("hidden", "expert", None),
        P("hidden", "expert", None),
        P("hidden", "expert", None),
        P("expert", None, "hidden"),
        P("expert", None, "hidden"),
        P("expert", "hidden", None),
    )
    out_specs = (
        P("hidden", "expert", None),
        P("hidden", "expert", None),
        P("expert", None, "hidden"),
        P("expert", None, "hidden"),
        P("expert", "hidden", None),
    )
    return jax.shard_map(
        on_device, mesh=mesh, in_specs=in_specs, out_specs=out_specs, check_vma=False
    )
```

```python
import functools

import jax
import jax.numpy as jnp
from jax import lax
from jax.experimental import pallas as pl
from jax.experimental.pallas import tpu as pltpu
from jax.sharding import PartitionSpec as P

TOP = 8
LANES = 128
BAND = 256
VMEM_ROWS = 24 * 2**20
VMEM_OUTER = 16 * 2**20
VMEM_SMALL = 4 * 2**20
IN_VMEM = pl.BlockSpec(memory_space=pltpu.VMEM)
IN_SMEM = pl.BlockSpec(memory_space=pltpu.SMEM)
IN_HBM = pl.BlockSpec(memory_space=pltpu.HBM)


def expert_core(x_rows, grad_rows, gate_col, gate_weight, up_weight, down_weight):
    pre_gate = jnp.dot(x_rows, gate_weight, preferred_element_type=jnp.float32)
    pre_up = jnp.dot(x_rows, up_weight, preferred_element_type=jnp.float32)
    back_grad = lax.dot_general(
        grad_rows, down_weight, (((1,), (1,)), ((), ())), preferred_element_type=jnp.float32
    )
    sigmoid_gate = jax.nn.sigmoid(pre_gate)
    silu_gate = pre_gate * sigmoid_gate
    active = silu_gate * pre_up
    gate_grad = jnp.sum(active * back_grad, axis=-1)
    weight = gate_col.astype(jnp.float32)
    scaled = (weight * active).astype(jnp.bfloat16)
    weighted_back = weight * back_grad
    d_gate_pre = (
        weighted_back * pre_up * sigmoid_gate * (1.0 + pre_gate * (1.0 - sigmoid_gate))
    ).astype(jnp.bfloat16)
    d_up_pre = (weighted_back * silu_gate).astype(jnp.bfloat16)
    sum_gate = lax.dot_general(
        x_rows, d_gate_pre, (((0,), (0,)), ((), ())), preferred_element_type=jnp.float32
    )
    sum_up = lax.dot_general(
        x_rows, d_up_pre, (((0,), (0,)), ((), ())), preferred_element_type=jnp.float32
    )
    sum_down = lax.dot_general(
        scaled, grad_rows, (((0,), (0,)), ((), ())), preferred_element_type=jnp.float32
    )
    return (gate_grad, d_gate_pre, d_up_pre, sum_gate, sum_up, sum_down)


def project_back(d_gate_pre, d_up_pre, gate_weight, up_weight):
    row_grad = lax.dot_general(
        d_gate_pre, gate_weight, (((1,), (1,)), ((), ())), preferred_element_type=jnp.float32
    )
    return row_grad + lax.dot_general(
        d_up_pre, up_weight, (((1,), (1,)), ((), ())), preferred_element_type=jnp.float32
    )


def routed_rows(tokens, grad_out, expert_ids, router_logits, w_gate, w_up, w_down):
    highest = lax.Precision.HIGHEST
    tok_dev = tokens.shape[1]
    peers = lax.axis_size("expert")
    mine = lax.axis_index("expert")
    row_cap = min(2 * tok_dev * TOP, tok_dev * peers)
    raised = jnp.exp(router_logits[0])
    gate_probs = raised / jnp.sum(raised, axis=-1, keepdims=True)
    gate_rows = gate_probs.astype(jnp.bfloat16)
    expert_range = jnp.arange(peers, dtype=jnp.int32)
    chosen = expert_ids[0][:, :, None] == expert_range[None, None, :]
    per_peer = jnp.sum(
        jnp.where(chosen, gate_rows.astype(jnp.float32)[:, :, None], jnp.float32(0.0)), axis=1
    )
    gate_table = per_peer.astype(jnp.bfloat16)
    got_x, got_grad, got_table = (
        lax.all_gather(tokens, "expert", axis=1, tiled=True),
        lax.all_gather(grad_out, "expert", axis=1, tiled=True),
        lax.all_gather(gate_table[None], "expert", axis=1, tiled=True),
    )
    all_x = got_x[0]
    all_grad = got_grad[0]
    column = jnp.sum(
        jnp.where(
            expert_range[None, :] == mine, got_table[0].astype(jnp.float32), jnp.float32(0.0)
        ),
        axis=-1,
    )
    picked = column > 0.0
    row_order = jnp.cumsum(picked.astype(jnp.int32)) - 1
    placing = (row_order[None, :] == jnp.arange(row_cap, dtype=jnp.int32)[:, None]) & picked[
        None, :
    ]
    placing_half = placing.astype(jnp.bfloat16)
    placing_full = placing.astype(jnp.float32)
    x_rows = jnp.dot(placing_half, all_x, preferred_element_type=jnp.float32).astype(jnp.bfloat16)
    grad_rows = jnp.dot(placing_half, all_grad, preferred_element_type=jnp.float32).astype(
        jnp.bfloat16
    )
    gate_col = jnp.dot(placing_full, column, precision=highest).astype(jnp.bfloat16)[:, None]
    gate_weight = w_gate[0]
    up_weight = w_up[0]
    down_weight = w_down[0]
    cycle_x, cycle_grad, cycle_gate = (
        lax.all_gather(x_rows, "hidden", axis=0, tiled=True),
        lax.all_gather(grad_rows, "hidden", axis=0, tiled=True),
        lax.all_gather(gate_col, "hidden", axis=0, tiled=True),
    )
    gate_part, gate_pre_all, up_pre_all, sum_gate, sum_up, sum_down = expert_core(
        cycle_x, cycle_grad, cycle_gate, gate_weight, up_weight, down_weight
    )
    row_part = project_back(gate_pre_all, up_pre_all, gate_weight, up_weight)
    own_rows, own_gate = (
        lax.psum_scatter(row_part, "hidden", scatter_dimension=0, tiled=True),
        lax.psum_scatter(gate_part, "hidden", scatter_dimension=0, tiled=True),
    )
    dense = lax.dot_general(placing_full, own_rows, (((0,), (0,)), ((), ())), precision=highest)
    token_gate = lax.dot_general(
        placing_full, own_gate, (((0,), (0,)), ((), ())), precision=highest
    )
    gate_out = jnp.where(expert_range[None, :] == mine, token_gate[:, None], jnp.float32(0.0))
    summed, gate_sums = (
        lax.psum_scatter(dense[None], "expert", scatter_dimension=1, tiled=True),
        lax.psum_scatter(gate_out[None], "expert", scatter_dimension=1, tiled=True),
    )
    gate_grad = jnp.sum(jnp.where(chosen, gate_sums[0][:, None, :], jnp.float32(0.0)), axis=-1)
    grad_logits = gate_probs * (gate_grad - jnp.sum(gate_probs * gate_grad, axis=-1, keepdims=True))
    return (summed, grad_logits[None], sum_gate[None], sum_up[None], sum_down[None])


def pack_kernel(tokens_ref, grads_ref, ids_ref, logits_ref, out_ref, ids_out, probs_out):
    depth = tokens_ref.shape[-1]
    tok_dev = tokens_ref.shape[1]
    raised = jnp.exp(logits_ref[0])
    probs = raised / jnp.sum(raised, axis=-1, keepdims=True)
    ids_out[...] = jnp.zeros_like(ids_out)
    probs_out[...] = jnp.zeros_like(probs_out)
    ids_out[:, :TOP] = ids_ref[0]
    probs_out[:, :TOP] = probs
    shares = probs.astype(jnp.bfloat16).astype(jnp.float32)
    ids = ids_ref[0]
    lane = lax.broadcasted_iota(jnp.int32, (tok_dev, LANES), 1)
    gates = jnp.zeros((tok_dev, LANES), jnp.float32)
    for k in range(TOP):
        gates = jnp.where(lane == ids[:, k : k + 1], shares[:, k : k + 1], gates)
    gates = gates.astype(jnp.bfloat16)
    tokens, grads = tokens_ref[0], grads_ref[0]
    for peer in range(out_ref.shape[0]):
        out_ref[peer, :, :depth] = tokens
        out_ref[peer, :, depth : 2 * depth] = grads
        out_ref[peer, :, 2 * depth :] = gates


def fetch_kernel(*refs):
    count = len(refs) // 2
    sems = refs[-1]
    copies = [
        pltpu.make_async_copy(refs[i], refs[count + i], sems.at[i]) for i in range(count)
    ]
    for copy in copies:
        copy.start()
    for copy in copies:
        copy.wait()


def rows_kernel(n_parts, place_ref, *refs):
    parts = refs[:n_parts]
    w_gate_ref, w_up_ref, w_down_ref = refs[n_parts : n_parts + 3]
    send_ref, x_ref, o_ref, scaled_ref, d_gate_ref, d_up_ref = refs[n_parts + 3 :]
    peers, tok_dev, width = parts[0].shape
    depth = x_ref.shape[1]
    each = peers * tok_dev
    mine, here = place_ref[0], place_ref[1]
    gates = []
    for s, part in enumerate(parts):
        rows = part[...].reshape(each, width)
        x_ref[s * each : (s + 1) * each, :] = rows[:, :depth]
        o_ref[s * each : (s + 1) * each, :] = rows[:, depth : 2 * depth]
        gates.append(rows[:, 2 * depth :].astype(jnp.float32))
    gates = jnp.concatenate(gates, axis=0)
    own_lane = lax.broadcasted_iota(jnp.int32, gates.shape, 1) == mine
    weight = jnp.sum(jnp.where(own_lane, gates, 0.0), axis=-1, keepdims=True)
    x_rows, grad_rows = x_ref[...], o_ref[...]
    pre_gate = jnp.dot(x_rows, w_gate_ref[0], preferred_element_type=jnp.float32)
    pre_up = jnp.dot(x_rows, w_up_ref[0], preferred_element_type=jnp.float32)
    across = (((1,), (1,)), ((), ()))
    back_grad = lax.dot_general(
        grad_rows, w_down_ref[0], across, preferred_element_type=jnp.float32
    )
    sigmoid_gate = 1.0 / (1.0 + jnp.exp(-pre_gate))
    silu_gate = pre_gate * sigmoid_gate
    active = silu_gate * pre_up
    gate_part = jnp.sum(active * back_grad, axis=-1, keepdims=True)
    weighted_back = weight * back_grad
    d_gate = (
        weighted_back * pre_up * sigmoid_gate * (1.0 + pre_gate * (1.0 - sigmoid_gate))
    ).astype(jnp.bfloat16)
    d_up = (weighted_back * silu_gate).astype(jnp.bfloat16)
    scaled_ref[...] = (weight * active).astype(jnp.bfloat16)
    d_gate_ref[...] = d_gate
    d_up_ref[...] = d_up
    row_grad = lax.dot_general(
        d_gate, w_gate_ref[0], across, preferred_element_type=jnp.float32
    ) + lax.dot_general(d_up, w_up_ref[0], across, preferred_element_type=jnp.float32)
    high = gate_part.astype(jnp.bfloat16).astype(jnp.float32)
    gate_high = jnp.where(own_lane, high, 0.0)
    gate_low = jnp.where(own_lane, gate_part - high, 0.0)
    for s in range(n_parts):
        owner = lax.rem(here + n_parts - s, n_parts)
        at = slice(s * each, (s + 1) * each)
        for value, start in ((row_grad, 0), (gate_high, depth), (gate_low, depth + LANES)):
            block = value[at].astype(jnp.bfloat16).reshape(peers, tok_dev, value.shape[1])
            send_ref[:, owner, :, start : start + value.shape[1]] = block


def outer_kernel(x_ref, o_ref, scaled_ref, d_gate_ref, d_up_ref, gate_ref, up_ref, down_ref):
    over_rows = (((0,), (0,)), ((), ()))
    x_rows = x_ref[...]
    gate_ref[0] = lax.dot_general(
        x_rows, d_gate_ref[...], over_rows, preferred_element_type=jnp.float32
    )
    up_ref[0] = lax.dot_general(
        x_rows, d_up_ref[...], over_rows, preferred_element_type=jnp.float32
    )
    down_ref[0] = lax.dot_general(
        scaled_ref[...], o_ref[...], over_rows, preferred_element_type=jnp.float32
    )


def finish_kernel(got_ref, ids_ref, probs_ref, grad_in_ref, grad_logits_ref):
    depth = grad_in_ref.shape[-1]
    total = got_ref[0].astype(jnp.float32)
    for block in range(1, got_ref.shape[0]):
        total = total + got_ref[block].astype(jnp.float32)
    grad_in_ref[0] = total[:, :depth]
    by_expert = total[:, depth : depth + LANES] + total[:, depth + LANES :]
    probs = probs_ref[...]
    gate_grad = jnp.take_along_axis(by_expert, ids_ref[...], axis=1)
    mean = jnp.sum(probs * gate_grad, axis=-1, keepdims=True)
    grad_logits_ref[0] = (probs * (gate_grad - mean))[:, :TOP]


def every_token(tokens, grad_out, expert_ids, router_logits, w_gate, w_up, w_down):
    peers, n_parts = lax.axis_size("expert"), lax.axis_size("hidden")
    tok_dev, depth = tokens.shape[1:]
    units = w_gate.shape[2]
    rows = n_parts * peers * tok_dev
    half = jnp.bfloat16
    shape = jax.ShapeDtypeStruct
    packed, ids, probs = pl.pallas_call(
        pack_kernel,
        in_specs=[IN_VMEM] * 4,
        out_specs=[IN_VMEM] * 3,
        out_shape=[
            shape((peers, tok_dev, 2 * depth + LANES), half),
            shape((tok_dev, LANES), jnp.int32),
            shape((tok_dev, LANES), jnp.float32),
        ],
        name="pack",
    )(tokens, grad_out, expert_ids, router_logits)
    parts = [lax.all_to_all(packed, "expert", 0, 0, tiled=True)]
    weights = (w_gate, w_up, w_down)
    fetched = pl.pallas_call(
        fetch_kernel,
        in_specs=[IN_HBM] * 3,
        out_specs=[IN_VMEM] * 3,
        out_shape=[pltpu.VMEM(w.shape, half) for w in weights],
        scratch_shapes=[pltpu.SemaphoreType.DMA((3,))],
        compiler_params=pltpu.CompilerParams(vmem_limit_bytes=VMEM_SMALL),
        cost_estimate=pl.CostEstimate(
            flops=0, bytes_accessed=12 * depth * units, transcendentals=0
        ),
        name="fetch",
    )(*[pltpu.with_memory_space_constraint(w, pltpu.HBM) for w in weights])
    for s in range(1, n_parts):
        turn = [(i, (i + s) % n_parts) for i in range(n_parts)]
        parts.append(lax.ppermute(parts[0], "hidden", turn))
    place = jnp.stack([lax.axis_index("expert"), lax.axis_index("hidden")]).astype(jnp.int32)
    products = 2 * rows * depth * units
    send, x_rows, grad_rows, scaled, d_gate, d_up = pl.pallas_call(
        functools.partial(rows_kernel, n_parts),
        in_specs=[IN_SMEM] + [IN_VMEM] * (n_parts + 3),
        out_specs=[IN_VMEM] * 6,
        out_shape=[
            shape((peers, n_parts, tok_dev, depth + 2 * LANES), half),
            shape((rows, depth), half),
            shape((rows, depth), half),
            shape((rows, units), half),
            shape((rows, units), half),
            shape((rows, units), half),
        ],
        compiler_params=pltpu.CompilerParams(vmem_limit_bytes=VMEM_ROWS),
        cost_estimate=pl.CostEstimate(
            flops=5 * products, bytes_accessed=6 * depth * units, transcendentals=rows * units
        ),
        name="rows",
    )(place, *parts, *fetched)
    send = send.reshape(peers * n_parts, tok_dev, depth + 2 * LANES)
    got = lax.all_to_all(send, ("expert", "hidden"), 0, 0, tiled=True)
    deep = min(BAND, depth)
    grad_gate, grad_up, grad_down = pl.pallas_call(
        outer_kernel,
        grid=(depth // deep,),
        in_specs=[
            pl.BlockSpec((rows, deep), lambda i: (0, i)),
            pl.BlockSpec((rows, deep), lambda i: (0, i)),
            pl.BlockSpec((rows, units), lambda i: (0, 0)),
            pl.BlockSpec((rows, units), lambda i: (0, 0)),
            pl.BlockSpec((rows, units), lambda i: (0, 0)),
        ],
        out_specs=[
            pl.BlockSpec((1, deep, units), lambda i: (0, i, 0)),
            pl.BlockSpec((1, deep, units), lambda i: (0, i, 0)),
            pl.BlockSpec((1, units, deep), lambda i: (0, 0, i)),
        ],
        out_shape=[
            shape((1, depth, units), jnp.float32),
            shape((1, depth, units), jnp.float32),
            shape((1, units, depth), jnp.float32),
        ],
        compiler_params=pltpu.CompilerParams(vmem_limit_bytes=VMEM_OUTER),
        cost_estimate=pl.CostEstimate(
            flops=3 * products, bytes_accessed=12 * depth * units, transcendentals=0
        ),
        name="outer",
    )(x_rows, grad_rows, scaled, d_gate, d_up)
    grad_in, grad_logits = pl.pallas_call(
        finish_kernel,
        in_specs=[IN_VMEM] * 3,
        out_specs=[IN_VMEM] * 2,
        out_shape=[
            shape((1, tok_dev, depth), jnp.float32),
            shape((1, tok_dev, TOP), jnp.float32),
        ],
        compiler_params=pltpu.CompilerParams(vmem_limit_bytes=VMEM_SMALL),
        name="finish",
    )(got, ids, probs)
    return grad_in, grad_logits, grad_gate, grad_up, grad_down


def on_device(tokens, grad_out, expert_ids, router_logits, w_gate, w_up, w_down):
    tok_dev, peers = tokens.shape[1], lax.axis_size("expert")
    most, there = 2 * tok_dev * TOP, tok_dev * peers
    whole_lanes = tokens.shape[2] % BAND == 0 and w_gate.shape[2] % LANES == 0
    plan = every_token if there <= most and peers <= LANES and whole_lanes else routed_rows
    return plan(tokens, grad_out, expert_ids, router_logits, w_gate, w_up, w_down)


def solution(mesh):
    in_specs = (
        P("hidden", "expert", None),
        P("hidden", "expert", None),
        P("hidden", "expert", None),
        P("hidden", "expert", None),
        P("expert", None, "hidden"),
        P("expert", None, "hidden"),
        P("expert", "hidden", None),
    )
    out_specs = (
        P("hidden", "expert", None),
        P("hidden", "expert", None),
        P("expert", None, "hidden"),
        P("expert", None, "hidden"),
        P("expert", "hidden", None),
    )
    return jax.shard_map(
        on_device, mesh=mesh, in_specs=in_specs, out_specs=out_specs, check_vma=False
    )
```

```python
import functools

import jax
import jax.numpy as jnp
from jax import lax
from jax.experimental import pallas as pl
from jax.experimental.pallas import tpu as pltpu
from jax.sharding import PartitionSpec as P

TOP = 8
LANES = 128
BAND = 256
DEPTH_AT_ONCE = 1024
VMEM_ROWS = 24 * 2**20
VMEM_OUTER = 24 * 2**20
VMEM_SMALL = 4 * 2**20
IN_VMEM = pl.BlockSpec(memory_space=pltpu.VMEM)
IN_HBM = pl.BlockSpec(memory_space=pltpu.HBM)


def expert_core(x_rows, grad_rows, gate_col, gate_weight, up_weight, down_weight):
    pre_gate = jnp.dot(x_rows, gate_weight, preferred_element_type=jnp.float32)
    pre_up = jnp.dot(x_rows, up_weight, preferred_element_type=jnp.float32)
    back_grad = lax.dot_general(
        grad_rows, down_weight, (((1,), (1,)), ((), ())), preferred_element_type=jnp.float32
    )
    sigmoid_gate = jax.nn.sigmoid(pre_gate)
    silu_gate = pre_gate * sigmoid_gate
    active = silu_gate * pre_up
    gate_grad = jnp.sum(active * back_grad, axis=-1)
    weight = gate_col.astype(jnp.float32)
    scaled = (weight * active).astype(jnp.bfloat16)
    weighted_back = weight * back_grad
    d_gate_pre = (
        weighted_back * pre_up * sigmoid_gate * (1.0 + pre_gate * (1.0 - sigmoid_gate))
    ).astype(jnp.bfloat16)
    d_up_pre = (weighted_back * silu_gate).astype(jnp.bfloat16)
    sum_gate = lax.dot_general(
        x_rows, d_gate_pre, (((0,), (0,)), ((), ())), preferred_element_type=jnp.float32
    )
    sum_up = lax.dot_general(
        x_rows, d_up_pre, (((0,), (0,)), ((), ())), preferred_element_type=jnp.float32
    )
    sum_down = lax.dot_general(
        scaled, grad_rows, (((0,), (0,)), ((), ())), preferred_element_type=jnp.float32
    )
    return (gate_grad, d_gate_pre, d_up_pre, sum_gate, sum_up, sum_down)


def project_back(d_gate_pre, d_up_pre, gate_weight, up_weight):
    row_grad = lax.dot_general(
        d_gate_pre, gate_weight, (((1,), (1,)), ((), ())), preferred_element_type=jnp.float32
    )
    return row_grad + lax.dot_general(
        d_up_pre, up_weight, (((1,), (1,)), ((), ())), preferred_element_type=jnp.float32
    )


def routed_rows(tokens, grad_out, expert_ids, router_logits, w_gate, w_up, w_down):
    highest = lax.Precision.HIGHEST
    tok_dev = tokens.shape[1]
    peers = lax.axis_size("expert")
    mine = lax.axis_index("expert")
    row_cap = min(2 * tok_dev * TOP, tok_dev * peers)
    raised = jnp.exp(router_logits[0])
    gate_probs = raised / jnp.sum(raised, axis=-1, keepdims=True)
    gate_rows = gate_probs.astype(jnp.bfloat16)
    expert_range = jnp.arange(peers, dtype=jnp.int32)
    chosen = expert_ids[0][:, :, None] == expert_range[None, None, :]
    per_peer = jnp.sum(
        jnp.where(chosen, gate_rows.astype(jnp.float32)[:, :, None], jnp.float32(0.0)), axis=1
    )
    gate_table = per_peer.astype(jnp.bfloat16)
    got_x, got_grad, got_table = (
        lax.all_gather(tokens, "expert", axis=1, tiled=True),
        lax.all_gather(grad_out, "expert", axis=1, tiled=True),
        lax.all_gather(gate_table[None], "expert", axis=1, tiled=True),
    )
    all_x = got_x[0]
    all_grad = got_grad[0]
    column = jnp.sum(
        jnp.where(
            expert_range[None, :] == mine, got_table[0].astype(jnp.float32), jnp.float32(0.0)
        ),
        axis=-1,
    )
    picked = column > 0.0
    row_order = jnp.cumsum(picked.astype(jnp.int32)) - 1
    placing = (row_order[None, :] == jnp.arange(row_cap, dtype=jnp.int32)[:, None]) & picked[
        None, :
    ]
    placing_half = placing.astype(jnp.bfloat16)
    placing_full = placing.astype(jnp.float32)
    x_rows = jnp.dot(placing_half, all_x, preferred_element_type=jnp.float32).astype(jnp.bfloat16)
    grad_rows = jnp.dot(placing_half, all_grad, preferred_element_type=jnp.float32).astype(
        jnp.bfloat16
    )
    gate_col = jnp.dot(placing_full, column, precision=highest).astype(jnp.bfloat16)[:, None]
    gate_weight = w_gate[0]
    up_weight = w_up[0]
    down_weight = w_down[0]
    cycle_x, cycle_grad, cycle_gate = (
        lax.all_gather(x_rows, "hidden", axis=0, tiled=True),
        lax.all_gather(grad_rows, "hidden", axis=0, tiled=True),
        lax.all_gather(gate_col, "hidden", axis=0, tiled=True),
    )
    gate_part, gate_pre_all, up_pre_all, sum_gate, sum_up, sum_down = expert_core(
        cycle_x, cycle_grad, cycle_gate, gate_weight, up_weight, down_weight
    )
    row_part = project_back(gate_pre_all, up_pre_all, gate_weight, up_weight)
    own_rows, own_gate = (
        lax.psum_scatter(row_part, "hidden", scatter_dimension=0, tiled=True),
        lax.psum_scatter(gate_part, "hidden", scatter_dimension=0, tiled=True),
    )
    dense = lax.dot_general(placing_full, own_rows, (((0,), (0,)), ((), ())), precision=highest)
    token_gate = lax.dot_general(
        placing_full, own_gate, (((0,), (0,)), ((), ())), precision=highest
    )
    gate_out = jnp.where(expert_range[None, :] == mine, token_gate[:, None], jnp.float32(0.0))
    summed, gate_sums = (
        lax.psum_scatter(dense[None], "expert", scatter_dimension=1, tiled=True),
        lax.psum_scatter(gate_out[None], "expert", scatter_dimension=1, tiled=True),
    )
    gate_grad = jnp.sum(jnp.where(chosen, gate_sums[0][:, None, :], jnp.float32(0.0)), axis=-1)
    grad_logits = gate_probs * (gate_grad - jnp.sum(gate_probs * gate_grad, axis=-1, keepdims=True))
    return (summed, grad_logits[None], sum_gate[None], sum_up[None], sum_down[None])


def gate_probs_of(logits):
    raised = jnp.exp(logits)
    return raised / jnp.sum(raised, axis=-1, keepdims=True)


def pack_kernel(tokens_ref, grads_ref, ids_ref, logits_ref, out_ref):
    tok_dev, depth = tokens_ref.shape[1:]
    shares = gate_probs_of(logits_ref[0]).astype(jnp.bfloat16).astype(jnp.float32)
    ids = ids_ref[0]
    lane = lax.broadcasted_iota(jnp.int32, (tok_dev, LANES), 1)
    gates = jnp.zeros((tok_dev, LANES), jnp.float32)
    for k in range(TOP):
        gates = jnp.where(lane == ids[:, k : k + 1], shares[:, k : k + 1], gates)
    gates = gates.astype(jnp.bfloat16)
    tokens, grads = tokens_ref[0], grads_ref[0]
    for peer in range(out_ref.shape[0]):
        out_ref[peer, :, :depth] = tokens
        out_ref[peer, :, depth : 2 * depth] = grads
        out_ref[peer, :, 2 * depth :] = gates


def fetch_kernel(count, *refs):
    sems = refs[-1]
    copies = [
        pltpu.make_async_copy(refs[i], refs[count + i], sems.at[i]) for i in range(count)
    ]
    for copy in copies:
        copy.start()
    for copy in copies:
        copy.wait()


def fetch(*arrays):
    size = sum(a.size * a.dtype.itemsize for a in arrays)
    count = len(arrays)
    return pl.pallas_call(
        functools.partial(fetch_kernel, count),
        in_specs=[IN_HBM] * count,
        out_specs=[IN_VMEM] * count,
        out_shape=[pltpu.VMEM(a.shape, a.dtype) for a in arrays],
        scratch_shapes=[pltpu.SemaphoreType.DMA((count,))],
        compiler_params=pltpu.CompilerParams(vmem_limit_bytes=VMEM_SMALL),
        cost_estimate=pl.CostEstimate(flops=0, bytes_accessed=2 * size, transcendentals=0),
        name="fetch",
    )(*[pltpu.with_memory_space_constraint(a, pltpu.HBM) for a in arrays])


def rows_kernel(n_parts, *refs):
    parts = refs[:n_parts]
    far_gate_ref, far_up_ref, w_down_ref = refs[n_parts : n_parts + 3]
    send_ref, x_ref, o_ref, scaled_ref, d_gate_ref, d_up_ref = refs[n_parts + 3 : n_parts + 9]
    w_gate_ref, w_up_ref, sems = refs[n_parts + 9 :]
    bring_gate = pltpu.make_async_copy(far_gate_ref, w_gate_ref, sems.at[0])
    bring_up = pltpu.make_async_copy(far_up_ref, w_up_ref, sems.at[1])
    bring_gate.start()
    peers, tok_dev, width = parts[0].shape
    depth = x_ref.shape[1]
    each = peers * tok_dev
    mine, here = lax.axis_index("expert"), lax.axis_index("hidden")
    gates = []
    for s, part in enumerate(parts):
        rows = part[...].reshape(each, width)
        x_ref[s * each : (s + 1) * each, :] = rows[:, :depth]
        o_ref[s * each : (s + 1) * each, :] = rows[:, depth : 2 * depth]
        gates.append(rows[:, 2 * depth :].astype(jnp.float32))
    bring_up.start()
    gates = jnp.concatenate(gates, axis=0)
    own_lane = lax.broadcasted_iota(jnp.int32, gates.shape, 1) == mine
    weight = jnp.sum(jnp.where(own_lane, gates, 0.0), axis=-1, keepdims=True)
    x_rows, grad_rows = x_ref[...], o_ref[...]
    across = (((1,), (1,)), ((), ()))
    back_grad = lax.dot_general(
        grad_rows, w_down_ref[0], across, preferred_element_type=jnp.float32
    )
    bring_gate.wait()
    pre_gate = jnp.dot(x_rows, w_gate_ref[0], preferred_element_type=jnp.float32)
    bring_up.wait()
    pre_up = jnp.dot(x_rows, w_up_ref[0], preferred_element_type=jnp.float32)
    sigmoid_gate = 1.0 / (1.0 + jnp.exp(-pre_gate))
    silu_gate = pre_gate * sigmoid_gate
    active = silu_gate * pre_up
    gate_part = jnp.sum(active * back_grad, axis=-1, keepdims=True)
    weighted_back = weight * back_grad
    d_gate = (
        weighted_back * pre_up * sigmoid_gate * (1.0 + pre_gate * (1.0 - sigmoid_gate))
    ).astype(jnp.bfloat16)
    d_up = (weighted_back * silu_gate).astype(jnp.bfloat16)
    scaled_ref[...] = (weight * active).astype(jnp.bfloat16)
    d_gate_ref[...] = d_gate
    d_up_ref[...] = d_up
    def put(value, start):
        for s in range(n_parts):
            owner = lax.rem(here + n_parts - s, n_parts)
            block = value[s * each : (s + 1) * each].astype(jnp.bfloat16)
            block = block.reshape(peers, tok_dev, value.shape[1])
            send_ref[:, owner, :, start : start + value.shape[1]] = block

    high = gate_part.astype(jnp.bfloat16).astype(jnp.float32)
    low_lane = lax.broadcasted_iota(jnp.int32, gates.shape, 1) == mine + LANES // 2
    low = jnp.where(low_lane, gate_part - high, 0.0)
    put(jnp.where(own_lane, high, low), depth)
    for start in range(0, depth, DEPTH_AT_ONCE):
        at = slice(start, min(start + DEPTH_AT_ONCE, depth))
        row_grad = lax.dot_general(
            w_gate_ref[0, at, :], d_gate, across, preferred_element_type=jnp.float32
        ) + lax.dot_general(
            w_up_ref[0, at, :], d_up, across, preferred_element_type=jnp.float32
        )
        put(row_grad.T, start)


def outer_kernel(
    x_ref, o_ref, scaled_ref, d_gate_ref, d_up_ref, ids_ref, logits_ref, *outs_and_scratch
):
    gate_ref, up_ref, down_ref, ids_out, probs_out = outs_and_scratch[:5]
    *held, ids_here, logits_here, sems, router_sems = outs_and_scratch[5:]
    router = [
        pltpu.make_async_copy(ids_ref, ids_here, router_sems.at[0]),
        pltpu.make_async_copy(logits_ref, logits_here, router_sems.at[1]),
    ]
    for copy in router:
        copy.start()
    over_rows = (((0,), (0,)), ((), ()))
    work = (
        (x_ref, d_gate_ref, gate_ref, held[0]),
        (x_ref, d_up_ref, up_ref, held[1]),
        (scaled_ref, o_ref, down_ref, held[2]),
    )
    copies = []
    for left, right, out, here in work:
        for start in range(0, left.shape[1], BAND):
            band = slice(start, min(start + BAND, left.shape[1]))
            here[band, :] = lax.dot_general(
                left[:, band], right[...], over_rows, preferred_element_type=jnp.float32
            )
            copy = pltpu.make_async_copy(
                here.at[band], out.at[0, band], sems.at[len(copies)]
            )
            copy.start()
            copies.append(copy)
    for copy in router:
        copy.wait()
    ids_out[...] = jnp.zeros_like(ids_out)
    ids_out[:, :TOP] = ids_here[0]
    probs_out[...] = jnp.zeros_like(probs_out)
    probs_out[:, :TOP] = gate_probs_of(logits_here[0])
    for copy in copies:
        copy.wait()


def finish_kernel(got_ref, ids_ref, probs_ref, grad_in_ref, grad_logits_ref):
    depth = grad_in_ref.shape[-1]
    total = got_ref[0].astype(jnp.float32)
    for block in range(1, got_ref.shape[0]):
        total = total + got_ref[block].astype(jnp.float32)
    grad_in_ref[0] = total[:, :depth]
    by_expert = total[:, depth:]
    probs, ids = probs_ref[...], ids_ref[...]
    gate_grad = jnp.take_along_axis(by_expert, ids, axis=1) + jnp.take_along_axis(
        by_expert, ids + LANES // 2, axis=1
    )
    mean = jnp.sum(probs * gate_grad, axis=-1, keepdims=True)
    grad_logits_ref[0] = (probs * (gate_grad - mean))[:, :TOP]


def every_token(tokens, grad_out, expert_ids, router_logits, w_gate, w_up, w_down):
    peers, n_parts = lax.axis_size("expert"), lax.axis_size("hidden")
    tok_dev, depth = tokens.shape[1:]
    units = w_gate.shape[2]
    rows = n_parts * peers * tok_dev
    half = jnp.bfloat16
    shape = jax.ShapeDtypeStruct
    packed = pl.pallas_call(
        pack_kernel,
        in_specs=[IN_VMEM] * 4,
        out_specs=IN_VMEM,
        out_shape=pltpu.VMEM((peers, tok_dev, 2 * depth + LANES), half),
        name="pack",
    )(tokens, grad_out, expert_ids, router_logits)
    parts = [lax.all_to_all(packed, "expert", 0, 0, tiled=True)]
    (w_down,) = fetch(w_down)
    for s in range(1, n_parts):
        turn = [(i, (i + s) % n_parts) for i in range(n_parts)]
        parts.append(lax.ppermute(parts[0], "hidden", turn))
    products = 2 * rows * depth * units
    send, x_rows, grad_rows, scaled, d_gate, d_up = pl.pallas_call(
        functools.partial(rows_kernel, n_parts),
        in_specs=[IN_VMEM] * n_parts + [IN_HBM] * 2 + [IN_VMEM],
        out_specs=[IN_VMEM] * 6,
        out_shape=[
            shape((peers, n_parts, tok_dev, depth + LANES), half),
            shape((rows, depth), half),
            shape((rows, depth), half),
            shape((rows, units), half),
            shape((rows, units), half),
            shape((rows, units), half),
        ],
        scratch_shapes=[
            pltpu.VMEM(w_gate.shape, half),
            pltpu.VMEM(w_up.shape, half),
            pltpu.SemaphoreType.DMA((2,)),
        ],
        compiler_params=pltpu.CompilerParams(vmem_limit_bytes=VMEM_ROWS),
        cost_estimate=pl.CostEstimate(
            flops=5 * products, bytes_accessed=6 * depth * units, transcendentals=rows * units
        ),
        name="rows",
    )(
        *parts,
        pltpu.with_memory_space_constraint(w_gate, pltpu.HBM),
        pltpu.with_memory_space_constraint(w_up, pltpu.HBM),
        w_down,
    )
    send = send.reshape(peers * n_parts, tok_dev, depth + LANES)
    got = lax.all_to_all(send, ("expert", "hidden"), 0, 0, tiled=True)
    bands = 2 * pl.cdiv(depth, BAND) + pl.cdiv(units, BAND)
    grad_gate, grad_up, grad_down, ids, probs = pl.pallas_call(
        outer_kernel,
        in_specs=[IN_VMEM] * 5 + [IN_HBM] * 2,
        out_specs=[IN_HBM] * 3 + [IN_VMEM] * 2,
        out_shape=[
            shape((1, depth, units), jnp.float32),
            shape((1, depth, units), jnp.float32),
            shape((1, units, depth), jnp.float32),
            shape((tok_dev, LANES), jnp.int32),
            shape((tok_dev, LANES), jnp.float32),
        ],
        scratch_shapes=[
            pltpu.VMEM((depth, units), jnp.float32),
            pltpu.VMEM((depth, units), jnp.float32),
            pltpu.VMEM((units, depth), jnp.float32),
            pltpu.VMEM(expert_ids.shape, expert_ids.dtype),
            pltpu.VMEM(router_logits.shape, router_logits.dtype),
            pltpu.SemaphoreType.DMA((bands,)),
            pltpu.SemaphoreType.DMA((2,)),
        ],
        compiler_params=pltpu.CompilerParams(vmem_limit_bytes=VMEM_OUTER),
        cost_estimate=pl.CostEstimate(
            flops=3 * products, bytes_accessed=12 * depth * units, transcendentals=0
        ),
        name="outer",
    )(
        x_rows,
        grad_rows,
        scaled,
        d_gate,
        d_up,
        pltpu.with_memory_space_constraint(expert_ids, pltpu.HBM),
        pltpu.with_memory_space_constraint(router_logits, pltpu.HBM),
    )
    grad_in, grad_logits = pl.pallas_call(
        finish_kernel,
        in_specs=[IN_VMEM] * 3,
        out_specs=[IN_VMEM] * 2,
        out_shape=[
            shape((1, tok_dev, depth), jnp.float32),
            shape((1, tok_dev, TOP), jnp.float32),
        ],
        compiler_params=pltpu.CompilerParams(vmem_limit_bytes=VMEM_SMALL),
        name="finish",
    )(got, ids, probs)
    return grad_in, grad_logits, grad_gate, grad_up, grad_down


def on_device(tokens, grad_out, expert_ids, router_logits, w_gate, w_up, w_down):
    tok_dev, peers = tokens.shape[1], lax.axis_size("expert")
    most, there = 2 * tok_dev * TOP, tok_dev * peers
    whole_lanes = tokens.shape[2] % BAND == 0 and w_gate.shape[2] % LANES == 0
    plan = every_token if there <= most and 2 * peers <= LANES and whole_lanes else routed_rows
    return plan(tokens, grad_out, expert_ids, router_logits, w_gate, w_up, w_down)


def solution(mesh):
    in_specs = (
        P("hidden", "expert", None),
        P("hidden", "expert", None),
        P("hidden", "expert", None),
        P("hidden", "expert", None),
        P("expert", None, "hidden"),
        P("expert", None, "hidden"),
        P("expert", "hidden", None),
    )
    out_specs = (
        P("hidden", "expert", None),
        P("hidden", "expert", None),
        P("expert", None, "hidden"),
        P("expert", None, "hidden"),
        P("expert", "hidden", None),
    )
    return jax.shard_map(
        on_device, mesh=mesh, in_specs=in_specs, out_specs=out_specs, check_vma=False
    )
```

```python
import functools

import jax
import jax.numpy as jnp
from jax import lax
from jax.experimental import pallas as pl
from jax.experimental.pallas import tpu as pltpu
from jax.sharding import PartitionSpec as P

TOP = 8
LANES = 128
BAND = 256
DEPTH_AT_ONCE = 1024
VMEM_ROWS = 24 * 2**20
VMEM_OUTER = 24 * 2**20
VMEM_SMALL = 4 * 2**20
IN_VMEM = pl.BlockSpec(memory_space=pltpu.VMEM)
ANYWHERE = pl.BlockSpec(memory_space=pl.ANY)
IN_HBM = pl.BlockSpec(memory_space=pltpu.HBM)


def expert_core(x_rows, grad_rows, gate_col, gate_weight, up_weight, down_weight):
    pre_gate = jnp.dot(x_rows, gate_weight, preferred_element_type=jnp.float32)
    pre_up = jnp.dot(x_rows, up_weight, preferred_element_type=jnp.float32)
    back_grad = lax.dot_general(
        grad_rows, down_weight, (((1,), (1,)), ((), ())), preferred_element_type=jnp.float32
    )
    sigmoid_gate = jax.nn.sigmoid(pre_gate)
    silu_gate = pre_gate * sigmoid_gate
    active = silu_gate * pre_up
    gate_grad = jnp.sum(active * back_grad, axis=-1)
    weight = gate_col.astype(jnp.float32)
    scaled = (weight * active).astype(jnp.bfloat16)
    weighted_back = weight * back_grad
    d_gate_pre = (
        weighted_back * pre_up * sigmoid_gate * (1.0 + pre_gate * (1.0 - sigmoid_gate))
    ).astype(jnp.bfloat16)
    d_up_pre = (weighted_back * silu_gate).astype(jnp.bfloat16)
    sum_gate = lax.dot_general(
        x_rows, d_gate_pre, (((0,), (0,)), ((), ())), preferred_element_type=jnp.float32
    )
    sum_up = lax.dot_general(
        x_rows, d_up_pre, (((0,), (0,)), ((), ())), preferred_element_type=jnp.float32
    )
    sum_down = lax.dot_general(
        scaled, grad_rows, (((0,), (0,)), ((), ())), preferred_element_type=jnp.float32
    )
    return (gate_grad, d_gate_pre, d_up_pre, sum_gate, sum_up, sum_down)


def project_back(d_gate_pre, d_up_pre, gate_weight, up_weight):
    row_grad = lax.dot_general(
        d_gate_pre, gate_weight, (((1,), (1,)), ((), ())), preferred_element_type=jnp.float32
    )
    return row_grad + lax.dot_general(
        d_up_pre, up_weight, (((1,), (1,)), ((), ())), preferred_element_type=jnp.float32
    )


def routed_rows(tokens, grad_out, expert_ids, router_logits, w_gate, w_up, w_down):
    highest = lax.Precision.HIGHEST
    tok_dev = tokens.shape[1]
    peers = lax.axis_size("expert")
    mine = lax.axis_index("expert")
    row_cap = min(2 * tok_dev * TOP, tok_dev * peers)
    raised = jnp.exp(router_logits[0])
    gate_probs = raised / jnp.sum(raised, axis=-1, keepdims=True)
    gate_rows = gate_probs.astype(jnp.bfloat16)
    expert_range = jnp.arange(peers, dtype=jnp.int32)
    chosen = expert_ids[0][:, :, None] == expert_range[None, None, :]
    per_peer = jnp.sum(
        jnp.where(chosen, gate_rows.astype(jnp.float32)[:, :, None], jnp.float32(0.0)), axis=1
    )
    gate_table = per_peer.astype(jnp.bfloat16)
    got_x, got_grad, got_table = (
        lax.all_gather(tokens, "expert", axis=1, tiled=True),
        lax.all_gather(grad_out, "expert", axis=1, tiled=True),
        lax.all_gather(gate_table[None], "expert", axis=1, tiled=True),
    )
    all_x = got_x[0]
    all_grad = got_grad[0]
    column = jnp.sum(
        jnp.where(
            expert_range[None, :] == mine, got_table[0].astype(jnp.float32), jnp.float32(0.0)
        ),
        axis=-1,
    )
    picked = column > 0.0
    row_order = jnp.cumsum(picked.astype(jnp.int32)) - 1
    placing = (row_order[None, :] == jnp.arange(row_cap, dtype=jnp.int32)[:, None]) & picked[
        None, :
    ]
    placing_half = placing.astype(jnp.bfloat16)
    placing_full = placing.astype(jnp.float32)
    x_rows = jnp.dot(placing_half, all_x, preferred_element_type=jnp.float32).astype(jnp.bfloat16)
    grad_rows = jnp.dot(placing_half, all_grad, preferred_element_type=jnp.float32).astype(
        jnp.bfloat16
    )
    gate_col = jnp.dot(placing_full, column, precision=highest).astype(jnp.bfloat16)[:, None]
    gate_weight = w_gate[0]
    up_weight = w_up[0]
    down_weight = w_down[0]
    cycle_x, cycle_grad, cycle_gate = (
        lax.all_gather(x_rows, "hidden", axis=0, tiled=True),
        lax.all_gather(grad_rows, "hidden", axis=0, tiled=True),
        lax.all_gather(gate_col, "hidden", axis=0, tiled=True),
    )
    gate_part, gate_pre_all, up_pre_all, sum_gate, sum_up, sum_down = expert_core(
        cycle_x, cycle_grad, cycle_gate, gate_weight, up_weight, down_weight
    )
    row_part = project_back(gate_pre_all, up_pre_all, gate_weight, up_weight)
    own_rows, own_gate = (
        lax.psum_scatter(row_part, "hidden", scatter_dimension=0, tiled=True),
        lax.psum_scatter(gate_part, "hidden", scatter_dimension=0, tiled=True),
    )
    dense = lax.dot_general(placing_full, own_rows, (((0,), (0,)), ((), ())), precision=highest)
    token_gate = lax.dot_general(
        placing_full, own_gate, (((0,), (0,)), ((), ())), precision=highest
    )
    gate_out = jnp.where(expert_range[None, :] == mine, token_gate[:, None], jnp.float32(0.0))
    summed, gate_sums = (
        lax.psum_scatter(dense[None], "expert", scatter_dimension=1, tiled=True),
        lax.psum_scatter(gate_out[None], "expert", scatter_dimension=1, tiled=True),
    )
    gate_grad = jnp.sum(jnp.where(chosen, gate_sums[0][:, None, :], jnp.float32(0.0)), axis=-1)
    grad_logits = gate_probs * (gate_grad - jnp.sum(gate_probs * gate_grad, axis=-1, keepdims=True))
    return (summed, grad_logits[None], sum_gate[None], sum_up[None], sum_down[None])


def gate_probs_of(logits):
    raised = jnp.exp(logits)
    return raised / jnp.sum(raised, axis=-1, keepdims=True)


def pack_kernel(tokens_ref, grads_ref, ids_ref, logits_ref, out_ref):
    tok_dev, depth = tokens_ref.shape[1:]
    shares = gate_probs_of(logits_ref[0]).astype(jnp.bfloat16).astype(jnp.float32)
    ids = ids_ref[0]
    lane = lax.broadcasted_iota(jnp.int32, (tok_dev, LANES), 1)
    gates = jnp.zeros((tok_dev, LANES), jnp.float32)
    for k in range(TOP):
        gates = jnp.where(lane == ids[:, k : k + 1], shares[:, k : k + 1], gates)
    gates = gates.astype(jnp.bfloat16)
    tokens, grads = tokens_ref[0], grads_ref[0]
    for peer in range(out_ref.shape[0]):
        out_ref[peer, :, :depth] = tokens
        out_ref[peer, :, depth : 2 * depth] = grads
        out_ref[peer, :, 2 * depth :] = gates


def fetch_kernel(count, *refs):
    sems = refs[-1]
    copies = [
        pltpu.make_async_copy(refs[i], refs[count + i], sems.at[i]) for i in range(count)
    ]
    for copy in copies:
        copy.start()
    for copy in copies:
        copy.wait()


def fetch(*arrays):
    size = sum(a.size * a.dtype.itemsize for a in arrays)
    count = len(arrays)
    return pl.pallas_call(
        functools.partial(fetch_kernel, count),
        in_specs=[IN_HBM] * count,
        out_specs=[IN_VMEM] * count,
        out_shape=[pltpu.VMEM(a.shape, a.dtype) for a in arrays],
        scratch_shapes=[pltpu.SemaphoreType.DMA((count,))],
        compiler_params=pltpu.CompilerParams(vmem_limit_bytes=VMEM_SMALL),
        cost_estimate=pl.CostEstimate(flops=0, bytes_accessed=2 * size, transcendentals=0),
        name="fetch",
    )(*[pltpu.with_memory_space_constraint(a, pltpu.HBM) for a in arrays])


def split_in_lanes(values):
    high = values.astype(jnp.bfloat16).astype(jnp.float32)
    return high + pltpu.roll(values - high, LANES // 2, 1)


def join_lanes(parts):
    lane = lax.broadcasted_iota(jnp.int32, parts.shape, 1)
    return jnp.where(lane < LANES // 2, parts + pltpu.roll(parts, LANES // 2, 1), 0.0)


def rows_kernel(n_parts, *refs):
    parts = refs[:n_parts]
    far_gate_ref, far_up_ref, w_down_ref = refs[n_parts : n_parts + 3]
    own_ref, x_ref, o_ref, scaled_ref, d_gate_ref, d_up_ref = refs[n_parts + 3 : n_parts + 9]
    other_refs = refs[n_parts + 9 : 2 * n_parts + 8]
    w_gate_ref, w_up_ref, sems = refs[2 * n_parts + 8 :]
    bring_gate = pltpu.make_async_copy(far_gate_ref, w_gate_ref, sems.at[0])
    bring_up = pltpu.make_async_copy(far_up_ref, w_up_ref, sems.at[1])
    bring_gate.start()
    peers, tok_dev, width = parts[0].shape
    depth = x_ref.shape[1]
    each = peers * tok_dev
    mine = lax.axis_index("expert")
    gates = []
    for s, part in enumerate(parts):
        rows = part[...].reshape(each, width)
        x_ref[s * each : (s + 1) * each, :] = rows[:, :depth]
        o_ref[s * each : (s + 1) * each, :] = rows[:, depth : 2 * depth]
        gates.append(rows[:, 2 * depth :].astype(jnp.float32))
    bring_up.start()
    gates = jnp.concatenate(gates, axis=0)
    own_lane = lax.broadcasted_iota(jnp.int32, gates.shape, 1) == mine
    weight = jnp.sum(jnp.where(own_lane, gates, 0.0), axis=-1, keepdims=True)
    x_rows, grad_rows = x_ref[...], o_ref[...]
    across = (((1,), (1,)), ((), ()))
    back_grad = lax.dot_general(
        grad_rows, w_down_ref[0], across, preferred_element_type=jnp.float32
    )
    bring_gate.wait()
    pre_gate = jnp.dot(x_rows, w_gate_ref[0], preferred_element_type=jnp.float32)
    bring_up.wait()
    pre_up = jnp.dot(x_rows, w_up_ref[0], preferred_element_type=jnp.float32)
    sigmoid_gate = 1.0 / (1.0 + jnp.exp(-pre_gate))
    silu_gate = pre_gate * sigmoid_gate
    active = silu_gate * pre_up
    gate_part = jnp.sum(active * back_grad, axis=-1, keepdims=True)
    weighted_back = weight * back_grad
    d_gate = (
        weighted_back * pre_up * sigmoid_gate * (1.0 + pre_gate * (1.0 - sigmoid_gate))
    ).astype(jnp.bfloat16)
    d_up = (weighted_back * silu_gate).astype(jnp.bfloat16)
    scaled_ref[...] = (weight * active).astype(jnp.bfloat16)
    d_gate_ref[...] = d_gate
    d_up_ref[...] = d_up
    def put(value, start):
        cols = slice(start, start + value.shape[1])
        own_ref[:, cols] = value[:each]
        for s, other in enumerate(other_refs, 1):
            block = value[s * each : (s + 1) * each].astype(jnp.bfloat16)
            other[:, :, cols] = block.reshape(peers, tok_dev, value.shape[1])

    put(split_in_lanes(jnp.where(own_lane, gate_part, 0.0)), depth)
    for start in range(0, depth, DEPTH_AT_ONCE):
        at = slice(start, min(start + DEPTH_AT_ONCE, depth))
        row_grad = lax.dot_general(
            w_gate_ref[0, at, :], d_gate, across, preferred_element_type=jnp.float32
        ) + lax.dot_general(
            w_up_ref[0, at, :], d_up, across, preferred_element_type=jnp.float32
        )
        put(row_grad.T, start)


def join_kernel(own_ref, *refs):
    send_ref = refs[-1]
    peers, tok_dev, width = send_ref.shape
    depth = width - LANES
    total, gates = own_ref[:, :depth], join_lanes(own_ref[:, depth:])
    for other in refs[:-1]:
        rows = other[...].reshape(peers * tok_dev, width).astype(jnp.float32)
        total, gates = total + rows[:, :depth], gates + join_lanes(rows[:, depth:])
    for value, cols in (
        (total, slice(0, depth)),
        (split_in_lanes(gates), slice(depth, width)),
    ):
        send_ref[:, :, cols] = value.astype(jnp.bfloat16).reshape(peers, tok_dev, value.shape[1])


def outer_kernel(
    after_ref,
    x_ref,
    o_ref,
    scaled_ref,
    d_gate_ref,
    d_up_ref,
    ids_ref,
    logits_ref,
    *outs_and_scratch,
):
    gate_ref, up_ref, down_ref, ids_out, probs_out = outs_and_scratch[:5]
    *held, ids_here, logits_here, sems, router_sems = outs_and_scratch[5:]
    router = [
        pltpu.make_async_copy(ids_ref, ids_here, router_sems.at[0]),
        pltpu.make_async_copy(logits_ref, logits_here, router_sems.at[1]),
    ]
    for copy in router:
        copy.start()
    over_rows = (((0,), (0,)), ((), ()))
    work = (
        (x_ref, d_gate_ref, gate_ref, held[0]),
        (x_ref, d_up_ref, up_ref, held[1]),
        (scaled_ref, o_ref, down_ref, held[2]),
    )
    copies = []
    for left, right, out, here in work:
        for start in range(0, left.shape[1], BAND):
            band = slice(start, min(start + BAND, left.shape[1]))
            here[band, :] = lax.dot_general(
                left[:, band], right[...], over_rows, preferred_element_type=jnp.float32
            )
            copy = pltpu.make_async_copy(
                here.at[band], out.at[0, band], sems.at[len(copies)]
            )
            copy.start()
            copies.append(copy)
    for copy in router:
        copy.wait()
    ids_out[...] = jnp.zeros_like(ids_out)
    ids_out[:, :TOP] = ids_here[0]
    probs_out[...] = jnp.zeros_like(probs_out)
    probs_out[:, :TOP] = gate_probs_of(logits_here[0])
    for copy in copies:
        copy.wait()


def finish_kernel(got_ref, ids_ref, probs_ref, grad_in_ref, grad_logits_ref):
    depth = grad_in_ref.shape[-1]
    total = got_ref[0].astype(jnp.float32)
    for block in range(1, got_ref.shape[0]):
        total = total + got_ref[block].astype(jnp.float32)
    grad_in_ref[0] = total[:, :depth]
    by_expert = total[:, depth:]
    probs, ids = probs_ref[...], ids_ref[...]
    gate_grad = jnp.take_along_axis(by_expert, ids, axis=1) + jnp.take_along_axis(
        by_expert, ids + LANES // 2, axis=1
    )
    mean = jnp.sum(probs * gate_grad, axis=-1, keepdims=True)
    grad_logits_ref[0] = (probs * (gate_grad - mean))[:, :TOP]


def every_token(tokens, grad_out, expert_ids, router_logits, w_gate, w_up, w_down):
    peers, n_parts = lax.axis_size("expert"), lax.axis_size("hidden")
    tok_dev, depth = tokens.shape[1:]
    units = w_gate.shape[2]
    rows = n_parts * peers * tok_dev
    half = jnp.bfloat16
    shape = jax.ShapeDtypeStruct
    packed = pl.pallas_call(
        pack_kernel,
        in_specs=[IN_VMEM] * 4,
        out_specs=IN_VMEM,
        out_shape=pltpu.VMEM((peers, tok_dev, 2 * depth + LANES), half),
        name="pack",
    )(tokens, grad_out, expert_ids, router_logits)
    parts = [lax.all_to_all(packed, "expert", 0, 0, tiled=True)]
    (w_down,) = fetch(w_down)
    for s in range(1, n_parts):
        turn = [(i, (i + s) % n_parts) for i in range(n_parts)]
        parts.append(lax.ppermute(parts[0], "hidden", turn))
    products = 2 * rows * depth * units
    own, x_rows, grad_rows, scaled, d_gate, d_up, *others = pl.pallas_call(
        functools.partial(rows_kernel, n_parts),
        in_specs=[IN_VMEM] * n_parts + [IN_HBM] * 2 + [IN_VMEM],
        out_specs=[IN_VMEM] * (n_parts + 5),
        out_shape=[
            shape((peers * tok_dev, depth + LANES), jnp.float32),
            shape((rows, depth), half),
            shape((rows, depth), half),
            shape((rows, units), half),
            shape((rows, units), half),
            shape((rows, units), half),
        ]
        + [shape((peers, tok_dev, depth + LANES), half)] * (n_parts - 1),
        scratch_shapes=[
            pltpu.VMEM(w_gate.shape, half),
            pltpu.VMEM(w_up.shape, half),
            pltpu.SemaphoreType.DMA((2,)),
        ],
        compiler_params=pltpu.CompilerParams(vmem_limit_bytes=VMEM_ROWS),
        cost_estimate=pl.CostEstimate(
            flops=5 * products, bytes_accessed=6 * depth * units, transcendentals=rows * units
        ),
        name="rows",
    )(
        *parts,
        pltpu.with_memory_space_constraint(w_gate, pltpu.HBM),
        pltpu.with_memory_space_constraint(w_up, pltpu.HBM),
        w_down,
    )
    for s in range(1, n_parts):
        turn = [(i, (i - s) % n_parts) for i in range(n_parts)]
        others[s - 1] = lax.ppermute(others[s - 1], "hidden", turn)
    send = pl.pallas_call(
        join_kernel,
        in_specs=[IN_VMEM] * n_parts,
        out_specs=IN_VMEM,
        out_shape=shape((peers, tok_dev, depth + LANES), half),
        compiler_params=pltpu.CompilerParams(vmem_limit_bytes=VMEM_SMALL),
        name="join",
    )(own, *others)
    got = lax.all_to_all(send, "expert", 0, 0, tiled=True)
    bands = 2 * pl.cdiv(depth, BAND) + pl.cdiv(units, BAND)
    grad_gate, grad_up, grad_down, ids, probs = pl.pallas_call(
        outer_kernel,
        in_specs=[ANYWHERE] + [IN_VMEM] * 5 + [IN_HBM] * 2,
        out_specs=[IN_HBM] * 3 + [IN_VMEM] * 2,
        out_shape=[
            shape((1, depth, units), jnp.float32),
            shape((1, depth, units), jnp.float32),
            shape((1, units, depth), jnp.float32),
            shape((tok_dev, LANES), jnp.int32),
            shape((tok_dev, LANES), jnp.float32),
        ],
        scratch_shapes=[
            pltpu.VMEM((depth, units), jnp.float32),
            pltpu.VMEM((depth, units), jnp.float32),
            pltpu.VMEM((units, depth), jnp.float32),
            pltpu.VMEM(expert_ids.shape, expert_ids.dtype),
            pltpu.VMEM(router_logits.shape, router_logits.dtype),
            pltpu.SemaphoreType.DMA((bands,)),
            pltpu.SemaphoreType.DMA((2,)),
        ],
        compiler_params=pltpu.CompilerParams(vmem_limit_bytes=VMEM_OUTER),
        cost_estimate=pl.CostEstimate(
            flops=3 * products, bytes_accessed=12 * depth * units, transcendentals=0
        ),
        name="outer",
    )(
        send,
        x_rows,
        grad_rows,
        scaled,
        d_gate,
        d_up,
        pltpu.with_memory_space_constraint(expert_ids, pltpu.HBM),
        pltpu.with_memory_space_constraint(router_logits, pltpu.HBM),
    )
    grad_in, grad_logits = pl.pallas_call(
        finish_kernel,
        in_specs=[IN_VMEM] * 3,
        out_specs=[IN_VMEM] * 2,
        out_shape=[
            shape((1, tok_dev, depth), jnp.float32),
            shape((1, tok_dev, TOP), jnp.float32),
        ],
        compiler_params=pltpu.CompilerParams(vmem_limit_bytes=VMEM_SMALL),
        name="finish",
    )(got, ids, probs)
    return grad_in, grad_logits, grad_gate, grad_up, grad_down


def on_device(tokens, grad_out, expert_ids, router_logits, w_gate, w_up, w_down):
    tok_dev, peers = tokens.shape[1], lax.axis_size("expert")
    most, there = 2 * tok_dev * TOP, tok_dev * peers
    whole_lanes = tokens.shape[2] % BAND == 0 and w_gate.shape[2] % LANES == 0
    plan = every_token if there <= most and 2 * peers <= LANES and whole_lanes else routed_rows
    return plan(tokens, grad_out, expert_ids, router_logits, w_gate, w_up, w_down)


def solution(mesh):
    in_specs = (
        P("hidden", "expert", None),
        P("hidden", "expert", None),
        P("hidden", "expert", None),
        P("hidden", "expert", None),
        P("expert", None, "hidden"),
        P("expert", None, "hidden"),
        P("expert", "hidden", None),
    )
    out_specs = (
        P("hidden", "expert", None),
        P("hidden", "expert", None),
        P("expert", None, "hidden"),
        P("expert", None, "hidden"),
        P("expert", "hidden", None),
    )
    return jax.shard_map(
        on_device, mesh=mesh, in_specs=in_specs, out_specs=out_specs, check_vma=False
    )
```

```python
import functools

import jax
import jax.numpy as jnp
from jax import lax
from jax.experimental import pallas as pl
from jax.experimental.pallas import tpu as pltpu
from jax.sharding import PartitionSpec as P

TOP = 8
LANES = 128
BAND = 256
DEPTH_AT_ONCE = 1024
VMEM_ROWS = 24 * 2**20
VMEM_OUTER = 24 * 2**20
VMEM_SMALL = 4 * 2**20
IN_VMEM = pl.BlockSpec(memory_space=pltpu.VMEM)
ANYWHERE = pl.BlockSpec(memory_space=pl.ANY)
IN_HBM = pl.BlockSpec(memory_space=pltpu.HBM)


def expert_core(x_rows, grad_rows, gate_col, gate_weight, up_weight, down_weight):
    pre_gate = jnp.dot(x_rows, gate_weight, preferred_element_type=jnp.float32)
    pre_up = jnp.dot(x_rows, up_weight, preferred_element_type=jnp.float32)
    back_grad = lax.dot_general(
        grad_rows, down_weight, (((1,), (1,)), ((), ())), preferred_element_type=jnp.float32
    )
    sigmoid_gate = jax.nn.sigmoid(pre_gate)
    silu_gate = pre_gate * sigmoid_gate
    active = silu_gate * pre_up
    gate_grad = jnp.sum(active * back_grad, axis=-1)
    weight = gate_col.astype(jnp.float32)
    scaled = (weight * active).astype(jnp.bfloat16)
    weighted_back = weight * back_grad
    d_gate_pre = (
        weighted_back * pre_up * sigmoid_gate * (1.0 + pre_gate * (1.0 - sigmoid_gate))
    ).astype(jnp.bfloat16)
    d_up_pre = (weighted_back * silu_gate).astype(jnp.bfloat16)
    sum_gate = lax.dot_general(
        x_rows, d_gate_pre, (((0,), (0,)), ((), ())), preferred_element_type=jnp.float32
    )
    sum_up = lax.dot_general(
        x_rows, d_up_pre, (((0,), (0,)), ((), ())), preferred_element_type=jnp.float32
    )
    sum_down = lax.dot_general(
        scaled, grad_rows, (((0,), (0,)), ((), ())), preferred_element_type=jnp.float32
    )
    return (gate_grad, d_gate_pre, d_up_pre, sum_gate, sum_up, sum_down)


def project_back(d_gate_pre, d_up_pre, gate_weight, up_weight):
    row_grad = lax.dot_general(
        d_gate_pre, gate_weight, (((1,), (1,)), ((), ())), preferred_element_type=jnp.float32
    )
    return row_grad + lax.dot_general(
        d_up_pre, up_weight, (((1,), (1,)), ((), ())), preferred_element_type=jnp.float32
    )


def routed_rows(tokens, grad_out, expert_ids, router_logits, w_gate, w_up, w_down):
    highest = lax.Precision.HIGHEST
    tok_dev = tokens.shape[1]
    peers = lax.axis_size("expert")
    mine = lax.axis_index("expert")
    row_cap = min(2 * tok_dev * TOP, tok_dev * peers)
    raised = jnp.exp(router_logits[0])
    gate_probs = raised / jnp.sum(raised, axis=-1, keepdims=True)
    gate_rows = gate_probs.astype(jnp.bfloat16)
    expert_range = jnp.arange(peers, dtype=jnp.int32)
    chosen = expert_ids[0][:, :, None] == expert_range[None, None, :]
    per_peer = jnp.sum(
        jnp.where(chosen, gate_rows.astype(jnp.float32)[:, :, None], jnp.float32(0.0)), axis=1
    )
    gate_table = per_peer.astype(jnp.bfloat16)
    got_x, got_grad, got_table = (
        lax.all_gather(tokens, "expert", axis=1, tiled=True),
        lax.all_gather(grad_out, "expert", axis=1, tiled=True),
        lax.all_gather(gate_table[None], "expert", axis=1, tiled=True),
    )
    all_x = got_x[0]
    all_grad = got_grad[0]
    column = jnp.sum(
        jnp.where(
            expert_range[None, :] == mine, got_table[0].astype(jnp.float32), jnp.float32(0.0)
        ),
        axis=-1,
    )
    picked = column > 0.0
    row_order = jnp.cumsum(picked.astype(jnp.int32)) - 1
    placing = (row_order[None, :] == jnp.arange(row_cap, dtype=jnp.int32)[:, None]) & picked[
        None, :
    ]
    placing_half = placing.astype(jnp.bfloat16)
    placing_full = placing.astype(jnp.float32)
    x_rows = jnp.dot(placing_half, all_x, preferred_element_type=jnp.float32).astype(jnp.bfloat16)
    grad_rows = jnp.dot(placing_half, all_grad, preferred_element_type=jnp.float32).astype(
        jnp.bfloat16
    )
    gate_col = jnp.dot(placing_full, column, precision=highest).astype(jnp.bfloat16)[:, None]
    gate_weight = w_gate[0]
    up_weight = w_up[0]
    down_weight = w_down[0]
    cycle_x, cycle_grad, cycle_gate = (
        lax.all_gather(x_rows, "hidden", axis=0, tiled=True),
        lax.all_gather(grad_rows, "hidden", axis=0, tiled=True),
        lax.all_gather(gate_col, "hidden", axis=0, tiled=True),
    )
    gate_part, gate_pre_all, up_pre_all, sum_gate, sum_up, sum_down = expert_core(
        cycle_x, cycle_grad, cycle_gate, gate_weight, up_weight, down_weight
    )
    row_part = project_back(gate_pre_all, up_pre_all, gate_weight, up_weight)
    own_rows, own_gate = (
        lax.psum_scatter(row_part, "hidden", scatter_dimension=0, tiled=True),
        lax.psum_scatter(gate_part, "hidden", scatter_dimension=0, tiled=True),
    )
    dense = lax.dot_general(placing_full, own_rows, (((0,), (0,)), ((), ())), precision=highest)
    token_gate = lax.dot_general(
        placing_full, own_gate, (((0,), (0,)), ((), ())), precision=highest
    )
    gate_out = jnp.where(expert_range[None, :] == mine, token_gate[:, None], jnp.float32(0.0))
    summed, gate_sums = (
        lax.psum_scatter(dense[None], "expert", scatter_dimension=1, tiled=True),
        lax.psum_scatter(gate_out[None], "expert", scatter_dimension=1, tiled=True),
    )
    gate_grad = jnp.sum(jnp.where(chosen, gate_sums[0][:, None, :], jnp.float32(0.0)), axis=-1)
    grad_logits = gate_probs * (gate_grad - jnp.sum(gate_probs * gate_grad, axis=-1, keepdims=True))
    return (summed, grad_logits[None], sum_gate[None], sum_up[None], sum_down[None])


def gate_probs_of(logits):
    raised = jnp.exp(logits)
    return raised / jnp.sum(raised, axis=-1, keepdims=True)


def pack_kernel(tokens_ref, grads_ref, ids_ref, logits_ref, out_ref):
    tok_dev, depth = tokens_ref.shape[1:]
    shares = gate_probs_of(logits_ref[0]).astype(jnp.bfloat16).astype(jnp.float32)
    ids = ids_ref[0]
    lane = lax.broadcasted_iota(jnp.int32, (tok_dev, LANES), 1)
    gates = jnp.zeros((tok_dev, LANES), jnp.float32)
    for k in range(TOP):
        gates = jnp.where(lane == ids[:, k : k + 1], shares[:, k : k + 1], gates)
    gates = gates.astype(jnp.bfloat16)
    tokens, grads = tokens_ref[0], grads_ref[0]
    for peer in range(out_ref.shape[0]):
        out_ref[peer, :, :depth] = tokens
        out_ref[peer, :, depth : 2 * depth] = grads
        out_ref[peer, :, 2 * depth :] = gates


def fetch_kernel(count, *refs):
    sems = refs[-1]
    copies = [
        pltpu.make_async_copy(refs[i], refs[count + i], sems.at[i]) for i in range(count)
    ]
    for copy in copies:
        copy.start()
    for copy in copies:
        copy.wait()


def fetch(*arrays):
    size = sum(a.size * a.dtype.itemsize for a in arrays)
    count = len(arrays)
    return pl.pallas_call(
        functools.partial(fetch_kernel, count),
        in_specs=[IN_HBM] * count,
        out_specs=[IN_VMEM] * count,
        out_shape=[pltpu.VMEM(a.shape, a.dtype) for a in arrays],
        scratch_shapes=[pltpu.SemaphoreType.DMA((count,))],
        compiler_params=pltpu.CompilerParams(vmem_limit_bytes=VMEM_SMALL),
        cost_estimate=pl.CostEstimate(flops=0, bytes_accessed=2 * size, transcendentals=0),
        name="fetch",
    )(*[pltpu.with_memory_space_constraint(a, pltpu.HBM) for a in arrays])


def split_in_lanes(values):
    high = values.astype(jnp.bfloat16).astype(jnp.float32)
    return high + pltpu.roll(values - high, LANES // 2, 1)


def join_lanes(parts):
    lane = lax.broadcasted_iota(jnp.int32, parts.shape, 1)
    return jnp.where(lane < LANES // 2, parts + pltpu.roll(parts, LANES // 2, 1), 0.0)


def rows_kernel(n_parts, *refs):
    parts = refs[:n_parts]
    far_gate_ref, far_up_ref, w_down_ref = refs[n_parts : n_parts + 3]
    own_ref, x_ref, o_ref, scaled_ref, d_gate_ref, d_up_ref = refs[n_parts + 3 : n_parts + 9]
    other_refs = refs[n_parts + 9 : 2 * n_parts + 8]
    w_gate_ref, w_up_ref, sems = refs[2 * n_parts + 8 :]
    bring_gate = pltpu.make_async_copy(far_gate_ref, w_gate_ref, sems.at[0])
    bring_up = pltpu.make_async_copy(far_up_ref, w_up_ref, sems.at[1])
    bring_gate.start()
    peers, tok_dev, width = parts[0].shape
    depth = x_ref.shape[1]
    each = peers * tok_dev
    mine = lax.axis_index("expert")
    gates = []
    for s, part in enumerate(parts):
        rows = part[...].reshape(each, width)
        x_ref[s * each : (s + 1) * each, :] = rows[:, :depth]
        o_ref[s * each : (s + 1) * each, :] = rows[:, depth : 2 * depth]
        gates.append(rows[:, 2 * depth :].astype(jnp.float32))
    bring_up.start()
    gates = jnp.concatenate(gates, axis=0)
    own_lane = lax.broadcasted_iota(jnp.int32, gates.shape, 1) == mine
    weight = jnp.sum(jnp.where(own_lane, gates, 0.0), axis=-1, keepdims=True)
    x_rows, grad_rows = x_ref[...], o_ref[...]
    across = (((1,), (1,)), ((), ()))
    back_grad = lax.dot_general(
        grad_rows, w_down_ref[0], across, preferred_element_type=jnp.float32
    )
    bring_gate.wait()
    pre_gate = jnp.dot(x_rows, w_gate_ref[0], preferred_element_type=jnp.float32)
    bring_up.wait()
    pre_up = jnp.dot(x_rows, w_up_ref[0], preferred_element_type=jnp.float32)
    sigmoid_gate = 1.0 / (1.0 + jnp.exp(-pre_gate))
    silu_gate = pre_gate * sigmoid_gate
    active = silu_gate * pre_up
    gate_part = jnp.sum(active * back_grad, axis=-1, keepdims=True)
    weighted_back = weight * back_grad
    d_gate = (
        weighted_back * pre_up * sigmoid_gate * (1.0 + pre_gate * (1.0 - sigmoid_gate))
    ).astype(jnp.bfloat16)
    d_up = (weighted_back * silu_gate).astype(jnp.bfloat16)
    scaled_ref[...] = (weight * active).astype(jnp.bfloat16)
    d_gate_ref[...] = d_gate
    d_up_ref[...] = d_up
    def put(value, start):
        cols = slice(start, start + value.shape[1])
        own_ref[:, cols] = value[:each]
        for s, other in enumerate(other_refs, 1):
            block = value[s * each : (s + 1) * each].astype(jnp.bfloat16)
            other[:, :, cols] = block.reshape(peers, tok_dev, value.shape[1])

    put(split_in_lanes(jnp.where(own_lane, gate_part, 0.0)), depth)
    for start in range(0, depth, DEPTH_AT_ONCE):
        at = slice(start, min(start + DEPTH_AT_ONCE, depth))
        row_grad = lax.dot_general(
            w_gate_ref[0, at, :], d_gate, across, preferred_element_type=jnp.float32
        ) + lax.dot_general(
            w_up_ref[0, at, :], d_up, across, preferred_element_type=jnp.float32
        )
        put(row_grad.T, start)


def join_kernel(own_ref, *refs):
    send_ref = refs[-1]
    peers, tok_dev, width = send_ref.shape
    depth = width - LANES
    total, gates = own_ref[:, :depth], join_lanes(own_ref[:, depth:])
    for other in refs[:-1]:
        rows = other[...].reshape(peers * tok_dev, width).astype(jnp.float32)
        total, gates = total + rows[:, :depth], gates + join_lanes(rows[:, depth:])
    for value, cols in (
        (total, slice(0, depth)),
        (split_in_lanes(gates), slice(depth, width)),
    ):
        send_ref[:, :, cols] = value.astype(jnp.bfloat16).reshape(peers, tok_dev, value.shape[1])


def outer_kernel(
    after_ref,
    x_ref,
    o_ref,
    scaled_ref,
    d_gate_ref,
    d_up_ref,
    ids_ref,
    logits_ref,
    *outs_and_scratch,
):
    gate_ref, up_ref, down_ref, ids_out, probs_out = outs_and_scratch[:5]
    *held, ids_here, logits_here, sems, router_sems = outs_and_scratch[5:]
    router = [
        pltpu.make_async_copy(ids_ref, ids_here, router_sems.at[0]),
        pltpu.make_async_copy(logits_ref, logits_here, router_sems.at[1]),
    ]
    for copy in router:
        copy.start()
    over_rows = (((0,), (0,)), ((), ()))
    work = (
        (x_ref, d_gate_ref, gate_ref, held[0]),
        (x_ref, d_up_ref, up_ref, held[1]),
        (scaled_ref, o_ref, down_ref, held[2]),
    )
    copies = []
    for left, right, out, here in work:
        for start in range(0, left.shape[1], BAND):
            band = slice(start, min(start + BAND, left.shape[1]))
            here[band, :] = lax.dot_general(
                left[:, band], right[...], over_rows, preferred_element_type=jnp.float32
            )
            copy = pltpu.make_async_copy(
                here.at[band], out.at[0, band], sems.at[len(copies)]
            )
            copy.start()
            copies.append(copy)
    for copy in router:
        copy.wait()
    ids_out[...] = jnp.zeros_like(ids_out)
    ids_out[:, :TOP] = ids_here[0]
    probs_out[...] = jnp.zeros_like(probs_out)
    probs_out[:, :TOP] = gate_probs_of(logits_here[0])
    for copy in copies:
        copy.wait()


def finish_kernel(got_ref, ids_ref, probs_ref, grad_in_ref, grad_logits_ref):
    depth = grad_in_ref.shape[-1]
    total = got_ref[0].astype(jnp.float32)
    for block in range(1, got_ref.shape[0]):
        total = total + got_ref[block].astype(jnp.float32)
    grad_in_ref[0] = total[:, :depth]
    by_expert = total[:, depth:]
    probs, ids = probs_ref[...], ids_ref[...]
    gate_grad = jnp.take_along_axis(by_expert, ids, axis=1) + jnp.take_along_axis(
        by_expert, ids + LANES // 2, axis=1
    )
    mean = jnp.sum(probs * gate_grad, axis=-1, keepdims=True)
    grad_logits_ref[0] = (probs * (gate_grad - mean))[:, :TOP]


def every_token(tokens, grad_out, expert_ids, router_logits, w_gate, w_up, w_down):
    peers, n_parts = lax.axis_size("expert"), lax.axis_size("hidden")
    tok_dev, depth = tokens.shape[1:]
    units = w_gate.shape[2]
    rows = n_parts * peers * tok_dev
    half = jnp.bfloat16
    shape = jax.ShapeDtypeStruct
    packed = pl.pallas_call(
        pack_kernel,
        in_specs=[IN_VMEM] * 4,
        out_specs=IN_VMEM,
        out_shape=pltpu.VMEM((peers, tok_dev, 2 * depth + LANES), half),
        name="pack",
    )(tokens, grad_out, expert_ids, router_logits)
    order = [[(peer + peers // 2) % peers for peer in range(peers)]]
    parts = [
        lax.all_to_all(packed, "expert", 0, 0, axis_index_groups=order, tiled=True)
    ]
    (w_down,) = fetch(w_down)
    for s in range(1, n_parts):
        turn = [(i, (i + s) % n_parts) for i in range(n_parts)]
        parts.append(lax.ppermute(parts[0], "hidden", turn))
    products = 2 * rows * depth * units
    own, x_rows, grad_rows, scaled, d_gate, d_up, *others = pl.pallas_call(
        functools.partial(rows_kernel, n_parts),
        in_specs=[IN_VMEM] * n_parts + [IN_HBM] * 2 + [IN_VMEM],
        out_specs=[IN_VMEM] * (n_parts + 5),
        out_shape=[
            shape((peers * tok_dev, depth + LANES), jnp.float32),
            shape((rows, depth), half),
            shape((rows, depth), half),
            shape((rows, units), half),
            shape((rows, units), half),
            shape((rows, units), half),
        ]
        + [shape((peers, tok_dev, depth + LANES), half)] * (n_parts - 1),
        scratch_shapes=[
            pltpu.VMEM(w_gate.shape, half),
            pltpu.VMEM(w_up.shape, half),
            pltpu.SemaphoreType.DMA((2,)),
        ],
        compiler_params=pltpu.CompilerParams(vmem_limit_bytes=VMEM_ROWS),
        cost_estimate=pl.CostEstimate(
            flops=5 * products, bytes_accessed=6 * depth * units, transcendentals=rows * units
        ),
        name="rows",
    )(
        *parts,
        pltpu.with_memory_space_constraint(w_gate, pltpu.HBM),
        pltpu.with_memory_space_constraint(w_up, pltpu.HBM),
        w_down,
    )
    for s in range(1, n_parts):
        turn = [(i, (i - s) % n_parts) for i in range(n_parts)]
        others[s - 1] = lax.ppermute(others[s - 1], "hidden", turn)
    send = pl.pallas_call(
        join_kernel,
        in_specs=[IN_VMEM] * n_parts,
        out_specs=IN_VMEM,
        out_shape=shape((peers, tok_dev, depth + LANES), half),
        compiler_params=pltpu.CompilerParams(vmem_limit_bytes=VMEM_SMALL),
        name="join",
    )(own, *others)
    got = lax.all_to_all(send, "expert", 0, 0, axis_index_groups=order, tiled=True)
    bands = 2 * pl.cdiv(depth, BAND) + pl.cdiv(units, BAND)
    grad_gate, grad_up, grad_down, ids, probs = pl.pallas_call(
        outer_kernel,
        in_specs=[ANYWHERE] + [IN_VMEM] * 5 + [IN_HBM] * 2,
        out_specs=[IN_HBM] * 3 + [IN_VMEM] * 2,
        out_shape=[
            shape((1, depth, units), jnp.float32),
            shape((1, depth, units), jnp.float32),
            shape((1, units, depth), jnp.float32),
            shape((tok_dev, LANES), jnp.int32),
            shape((tok_dev, LANES), jnp.float32),
        ],
        scratch_shapes=[
            pltpu.VMEM((depth, units), jnp.float32),
            pltpu.VMEM((depth, units), jnp.float32),
            pltpu.VMEM((units, depth), jnp.float32),
            pltpu.VMEM(expert_ids.shape, expert_ids.dtype),
            pltpu.VMEM(router_logits.shape, router_logits.dtype),
            pltpu.SemaphoreType.DMA((bands,)),
            pltpu.SemaphoreType.DMA((2,)),
        ],
        compiler_params=pltpu.CompilerParams(vmem_limit_bytes=VMEM_OUTER),
        cost_estimate=pl.CostEstimate(
            flops=3 * products, bytes_accessed=12 * depth * units, transcendentals=0
        ),
        name="outer",
    )(
        send,
        x_rows,
        grad_rows,
        scaled,
        d_gate,
        d_up,
        pltpu.with_memory_space_constraint(expert_ids, pltpu.HBM),
        pltpu.with_memory_space_constraint(router_logits, pltpu.HBM),
    )
    grad_in, grad_logits = pl.pallas_call(
        finish_kernel,
        in_specs=[IN_VMEM] * 3,
        out_specs=[IN_VMEM] * 2,
        out_shape=[
            shape((1, tok_dev, depth), jnp.float32),
            shape((1, tok_dev, TOP), jnp.float32),
        ],
        compiler_params=pltpu.CompilerParams(vmem_limit_bytes=VMEM_SMALL),
        name="finish",
    )(got, ids, probs)
    return grad_in, grad_logits, grad_gate, grad_up, grad_down


def on_device(tokens, grad_out, expert_ids, router_logits, w_gate, w_up, w_down):
    tok_dev, peers = tokens.shape[1], lax.axis_size("expert")
    most, there = 2 * tok_dev * TOP, tok_dev * peers
    whole_lanes = tokens.shape[2] % BAND == 0 and w_gate.shape[2] % LANES == 0
    plan = every_token if there <= most and 2 * peers <= LANES and whole_lanes else routed_rows
    return plan(tokens, grad_out, expert_ids, router_logits, w_gate, w_up, w_down)


def solution(mesh):
    in_specs = (
        P("hidden", "expert", None),
        P("hidden", "expert", None),
        P("hidden", "expert", None),
        P("hidden", "expert", None),
        P("expert", None, "hidden"),
        P("expert", None, "hidden"),
        P("expert", "hidden", None),
    )
    out_specs = (
        P("hidden", "expert", None),
        P("hidden", "expert", None),
        P("expert", None, "hidden"),
        P("expert", None, "hidden"),
        P("expert", "hidden", None),
    )
    return jax.shard_map(
        on_device, mesh=mesh, in_specs=in_specs, out_specs=out_specs, check_vma=False
    )
```

```python
import functools

import jax
import jax.numpy as jnp
from jax import lax
from jax.experimental import pallas as pl
from jax.experimental.pallas import tpu as pltpu
from jax.sharding import PartitionSpec as P

TOP = 8
LANES = 128
BAND = 512
DEPTH_AT_ONCE = 1024
VMEM_ROWS = 24 * 2**20
VMEM_OUTER = 24 * 2**20
VMEM_SMALL = 4 * 2**20
IN_VMEM = pl.BlockSpec(memory_space=pltpu.VMEM)
ANYWHERE = pl.BlockSpec(memory_space=pl.ANY)
IN_HBM = pl.BlockSpec(memory_space=pltpu.HBM)


def expert_core(x_rows, grad_rows, gate_col, gate_weight, up_weight, down_weight):
    pre_gate = jnp.dot(x_rows, gate_weight, preferred_element_type=jnp.float32)
    pre_up = jnp.dot(x_rows, up_weight, preferred_element_type=jnp.float32)
    back_grad = lax.dot_general(
        grad_rows, down_weight, (((1,), (1,)), ((), ())), preferred_element_type=jnp.float32
    )
    sigmoid_gate = jax.nn.sigmoid(pre_gate)
    silu_gate = pre_gate * sigmoid_gate
    active = silu_gate * pre_up
    gate_grad = jnp.sum(active * back_grad, axis=-1)
    weight = gate_col.astype(jnp.float32)
    scaled = (weight * active).astype(jnp.bfloat16)
    weighted_back = weight * back_grad
    d_gate_pre = (
        weighted_back * pre_up * sigmoid_gate * (1.0 + pre_gate * (1.0 - sigmoid_gate))
    ).astype(jnp.bfloat16)
    d_up_pre = (weighted_back * silu_gate).astype(jnp.bfloat16)
    sum_gate = lax.dot_general(
        x_rows, d_gate_pre, (((0,), (0,)), ((), ())), preferred_element_type=jnp.float32
    )
    sum_up = lax.dot_general(
        x_rows, d_up_pre, (((0,), (0,)), ((), ())), preferred_element_type=jnp.float32
    )
    sum_down = lax.dot_general(
        scaled, grad_rows, (((0,), (0,)), ((), ())), preferred_element_type=jnp.float32
    )
    return (gate_grad, d_gate_pre, d_up_pre, sum_gate, sum_up, sum_down)


def project_back(d_gate_pre, d_up_pre, gate_weight, up_weight):
    row_grad = lax.dot_general(
        d_gate_pre, gate_weight, (((1,), (1,)), ((), ())), preferred_element_type=jnp.float32
    )
    return row_grad + lax.dot_general(
        d_up_pre, up_weight, (((1,), (1,)), ((), ())), preferred_element_type=jnp.float32
    )


def routed_rows(tokens, grad_out, expert_ids, router_logits, w_gate, w_up, w_down):
    highest = lax.Precision.HIGHEST
    tok_dev = tokens.shape[1]
    peers = lax.axis_size("expert")
    mine = lax.axis_index("expert")
    row_cap = min(2 * tok_dev * TOP, tok_dev * peers)
    raised = jnp.exp(router_logits[0])
    gate_probs = raised / jnp.sum(raised, axis=-1, keepdims=True)
    gate_rows = gate_probs.astype(jnp.bfloat16)
    expert_range = jnp.arange(peers, dtype=jnp.int32)
    chosen = expert_ids[0][:, :, None] == expert_range[None, None, :]
    per_peer = jnp.sum(
        jnp.where(chosen, gate_rows.astype(jnp.float32)[:, :, None], jnp.float32(0.0)), axis=1
    )
    gate_table = per_peer.astype(jnp.bfloat16)
    got_x, got_grad, got_table = (
        lax.all_gather(tokens, "expert", axis=1, tiled=True),
        lax.all_gather(grad_out, "expert", axis=1, tiled=True),
        lax.all_gather(gate_table[None], "expert", axis=1, tiled=True),
    )
    all_x = got_x[0]
    all_grad = got_grad[0]
    column = jnp.sum(
        jnp.where(
            expert_range[None, :] == mine, got_table[0].astype(jnp.float32), jnp.float32(0.0)
        ),
        axis=-1,
    )
    picked = column > 0.0
    row_order = jnp.cumsum(picked.astype(jnp.int32)) - 1
    placing = (row_order[None, :] == jnp.arange(row_cap, dtype=jnp.int32)[:, None]) & picked[
        None, :
    ]
    placing_half = placing.astype(jnp.bfloat16)
    placing_full = placing.astype(jnp.float32)
    x_rows = jnp.dot(placing_half, all_x, preferred_element_type=jnp.float32).astype(jnp.bfloat16)
    grad_rows = jnp.dot(placing_half, all_grad, preferred_element_type=jnp.float32).astype(
        jnp.bfloat16
    )
    gate_col = jnp.dot(placing_full, column, precision=highest).astype(jnp.bfloat16)[:, None]
    gate_weight = w_gate[0]
    up_weight = w_up[0]
    down_weight = w_down[0]
    cycle_x, cycle_grad, cycle_gate = (
        lax.all_gather(x_rows, "hidden", axis=0, tiled=True),
        lax.all_gather(grad_rows, "hidden", axis=0, tiled=True),
        lax.all_gather(gate_col, "hidden", axis=0, tiled=True),
    )
    gate_part, gate_pre_all, up_pre_all, sum_gate, sum_up, sum_down = expert_core(
        cycle_x, cycle_grad, cycle_gate, gate_weight, up_weight, down_weight
    )
    row_part = project_back(gate_pre_all, up_pre_all, gate_weight, up_weight)
    own_rows, own_gate = (
        lax.psum_scatter(row_part, "hidden", scatter_dimension=0, tiled=True),
        lax.psum_scatter(gate_part, "hidden", scatter_dimension=0, tiled=True),
    )
    dense = lax.dot_general(placing_full, own_rows, (((0,), (0,)), ((), ())), precision=highest)
    token_gate = lax.dot_general(
        placing_full, own_gate, (((0,), (0,)), ((), ())), precision=highest
    )
    gate_out = jnp.where(expert_range[None, :] == mine, token_gate[:, None], jnp.float32(0.0))
    summed, gate_sums = (
        lax.psum_scatter(dense[None], "expert", scatter_dimension=1, tiled=True),
        lax.psum_scatter(gate_out[None], "expert", scatter_dimension=1, tiled=True),
    )
    gate_grad = jnp.sum(jnp.where(chosen, gate_sums[0][:, None, :], jnp.float32(0.0)), axis=-1)
    grad_logits = gate_probs * (gate_grad - jnp.sum(gate_probs * gate_grad, axis=-1, keepdims=True))
    return (summed, grad_logits[None], sum_gate[None], sum_up[None], sum_down[None])


def gate_probs_of(logits):
    raised = jnp.exp(logits)
    return raised / jnp.sum(raised, axis=-1, keepdims=True)


def pack_kernel(tokens_ref, grads_ref, ids_ref, logits_ref, out_ref):
    tok_dev, depth = tokens_ref.shape[1:]
    shares = gate_probs_of(logits_ref[0]).astype(jnp.bfloat16).astype(jnp.float32)
    ids = ids_ref[0]
    lane = lax.broadcasted_iota(jnp.int32, (tok_dev, LANES), 1)
    gates = jnp.zeros((tok_dev, LANES), jnp.float32)
    for k in range(TOP):
        gates = jnp.where(lane == ids[:, k : k + 1], shares[:, k : k + 1], gates)
    gates = gates.astype(jnp.bfloat16)
    tokens, grads = tokens_ref[0], grads_ref[0]
    for peer in range(out_ref.shape[0]):
        out_ref[peer, :, :depth] = tokens
        out_ref[peer, :, depth : 2 * depth] = grads
        out_ref[peer, :, 2 * depth :] = gates


def fetch_kernel(last, far_ref, *refs):
    here_ref, sem = refs[-2:]
    on_last = lax.axis_index("hidden") == lax.axis_size("hidden") - 1

    @pl.when(on_last if last else jnp.logical_not(on_last))
    def _():
        copy = pltpu.make_async_copy(far_ref, here_ref, sem)
        copy.start()
        copy.wait()


def fetch(last, array, held, aliases):
    spec = [IN_HBM, ANYWHERE if last else IN_VMEM]
    here = pltpu.VMEM(array.shape, array.dtype)
    out = pl.pallas_call(
        functools.partial(fetch_kernel, last),
        in_specs=spec,
        out_specs=[ANYWHERE, IN_VMEM] if last else IN_VMEM,
        out_shape=[jax.ShapeDtypeStruct(held.shape, held.dtype), here] if last else here,
        input_output_aliases=aliases,
        scratch_shapes=[pltpu.SemaphoreType.DMA],
        compiler_params=pltpu.CompilerParams(vmem_limit_bytes=VMEM_SMALL),
        cost_estimate=pl.CostEstimate(
            flops=0, bytes_accessed=2 * array.size * array.dtype.itemsize, transcendentals=0
        ),
        name="fetch",
    )(array, held)
    return out


def split_in_lanes(values):
    high = values.astype(jnp.bfloat16).astype(jnp.float32)
    return high + pltpu.roll(values - high, LANES // 2, 1)


def join_lanes(parts):
    lane = lax.broadcasted_iota(jnp.int32, parts.shape, 1)
    return jnp.where(lane < LANES // 2, parts + pltpu.roll(parts, LANES // 2, 1), 0.0)


def rows_kernel(n_parts, *refs):
    parts = refs[:n_parts]
    far_gate_ref, far_up_ref, w_down_ref = refs[n_parts : n_parts + 3]
    own_ref, x_ref, o_ref, scaled_ref, d_gate_ref, d_up_ref = refs[n_parts + 3 : n_parts + 9]
    other_refs = refs[n_parts + 9 : 2 * n_parts + 8]
    w_gate_ref, w_up_ref, sems = refs[2 * n_parts + 8 :]
    bring_gate = pltpu.make_async_copy(far_gate_ref, w_gate_ref, sems.at[0])
    bring_up = pltpu.make_async_copy(far_up_ref, w_up_ref, sems.at[1])
    bring_gate.start()
    peers, tok_dev, width = parts[0].shape
    depth = x_ref.shape[1]
    each = peers * tok_dev
    mine = lax.axis_index("expert")
    gates = []
    for s, part in enumerate(parts):
        rows = part[...].reshape(each, width)
        x_ref[s * each : (s + 1) * each, :] = rows[:, :depth]
        o_ref[s * each : (s + 1) * each, :] = rows[:, depth : 2 * depth]
        gates.append(rows[:, 2 * depth :].astype(jnp.float32))
    bring_up.start()
    gates = jnp.concatenate(gates, axis=0)
    own_lane = lax.broadcasted_iota(jnp.int32, gates.shape, 1) == mine
    weight = jnp.sum(jnp.where(own_lane, gates, 0.0), axis=-1, keepdims=True)
    x_rows, grad_rows = x_ref[...], o_ref[...]
    across = (((1,), (1,)), ((), ()))
    back_grad = lax.dot_general(
        grad_rows, w_down_ref[0], across, preferred_element_type=jnp.float32
    )
    bring_gate.wait()
    pre_gate = jnp.dot(x_rows, w_gate_ref[0], preferred_element_type=jnp.float32)
    bring_up.wait()
    pre_up = jnp.dot(x_rows, w_up_ref[0], preferred_element_type=jnp.float32)
    sigmoid_gate = 1.0 / (1.0 + jnp.exp(-pre_gate))
    silu_gate = pre_gate * sigmoid_gate
    active = silu_gate * pre_up
    gate_part = jnp.sum(active * back_grad, axis=-1, keepdims=True)
    weighted_back = weight * back_grad
    d_gate = (
        weighted_back * pre_up * sigmoid_gate * (1.0 + pre_gate * (1.0 - sigmoid_gate))
    ).astype(jnp.bfloat16)
    d_up = (weighted_back * silu_gate).astype(jnp.bfloat16)
    scaled_ref[...] = (weight * active).astype(jnp.bfloat16)
    d_gate_ref[...] = d_gate
    d_up_ref[...] = d_up
    def put(value, start):
        cols = slice(start, start + value.shape[1])
        own_ref[:, cols] = value[:each]
        for s, other in enumerate(other_refs, 1):
            block = value[s * each : (s + 1) * each].astype(jnp.bfloat16)
            other[:, :, cols] = block.reshape(peers, tok_dev, value.shape[1])

    put(split_in_lanes(jnp.where(own_lane, gate_part, 0.0)), depth)
    for start in range(0, depth, DEPTH_AT_ONCE):
        at = slice(start, min(start + DEPTH_AT_ONCE, depth))
        row_grad = lax.dot_general(
            w_gate_ref[0, at, :], d_gate, across, preferred_element_type=jnp.float32
        ) + lax.dot_general(
            w_up_ref[0, at, :], d_up, across, preferred_element_type=jnp.float32
        )
        put(row_grad.T, start)


def join_kernel(own_ref, *refs):
    send_ref = refs[-1]
    peers, tok_dev, width = send_ref.shape
    depth = width - LANES
    total, gates = own_ref[:, :depth], join_lanes(own_ref[:, depth:])
    for other in refs[:-1]:
        rows = other[...].reshape(peers * tok_dev, width).astype(jnp.float32)
        total, gates = total + rows[:, :depth], gates + join_lanes(rows[:, depth:])
    for value, cols in (
        (total, slice(0, depth)),
        (split_in_lanes(gates), slice(depth, width)),
    ):
        send_ref[:, :, cols] = value.astype(jnp.bfloat16).reshape(peers, tok_dev, value.shape[1])


def outer_kernel(
    after_ref,
    x_ref,
    o_ref,
    scaled_ref,
    d_gate_ref,
    d_up_ref,
    ids_ref,
    logits_ref,
    *outs_and_scratch,
):
    gate_ref, up_ref, down_ref, ids_out, probs_out = outs_and_scratch[:5]
    *held, ids_here, logits_here, sems, router_sems = outs_and_scratch[5:]
    router = [
        pltpu.make_async_copy(ids_ref, ids_here, router_sems.at[0]),
        pltpu.make_async_copy(logits_ref, logits_here, router_sems.at[1]),
    ]
    for copy in router:
        copy.start()
    over_rows = (((0,), (0,)), ((), ()))
    work = (
        (x_ref, d_gate_ref, gate_ref, held[0]),
        (x_ref, d_up_ref, up_ref, held[1]),
        (scaled_ref, o_ref, down_ref, held[2]),
    )
    copies = []
    for left, right, out, here in work:
        end = left.shape[1]
        edges = sorted({0, min(LANES, end), *range(BAND, end, BAND), end})
        for band in (slice(*pair) for pair in zip(edges, edges[1:])):
            here[band, :] = lax.dot_general(
                left[:, band], right[...], over_rows, preferred_element_type=jnp.float32
            )
            copy = pltpu.make_async_copy(
                here.at[band], out.at[0, band], sems.at[len(copies)]
            )
            copy.start()
            copies.append(copy)
    for copy in router:
        copy.wait()
    ids_out[...] = jnp.zeros_like(ids_out)
    ids_out[:, :TOP] = ids_here[0]
    probs_out[...] = jnp.zeros_like(probs_out)
    probs_out[:, :TOP] = gate_probs_of(logits_here[0])
    for copy in copies:
        copy.wait()


def finish_kernel(got_ref, ids_ref, probs_ref, grad_in_ref, grad_logits_ref):
    depth = grad_in_ref.shape[-1]
    total = got_ref[0].astype(jnp.float32)
    for block in range(1, got_ref.shape[0]):
        total = total + got_ref[block].astype(jnp.float32)
    grad_in_ref[0] = total[:, :depth]
    by_expert = total[:, depth:]
    probs, ids = probs_ref[...], ids_ref[...]
    gate_grad = jnp.take_along_axis(by_expert, ids, axis=1) + jnp.take_along_axis(
        by_expert, ids + LANES // 2, axis=1
    )
    mean = jnp.sum(probs * gate_grad, axis=-1, keepdims=True)
    grad_logits_ref[0] = (probs * (gate_grad - mean))[:, :TOP]


def every_token(tokens, grad_out, expert_ids, router_logits, w_gate, w_up, w_down):
    peers, n_parts = lax.axis_size("expert"), lax.axis_size("hidden")
    tok_dev, depth = tokens.shape[1:]
    units = w_gate.shape[2]
    rows = n_parts * peers * tok_dev
    half = jnp.bfloat16
    shape = jax.ShapeDtypeStruct
    packed = pl.pallas_call(
        pack_kernel,
        in_specs=[IN_VMEM] * 4,
        out_specs=IN_VMEM,
        out_shape=pltpu.VMEM((peers, tok_dev, 2 * depth + LANES), half),
        name="pack",
    )(tokens, grad_out, expert_ids, router_logits)
    order = [[(peer + peers // 2) % peers for peer in range(peers)]]
    parts = [
        lax.all_to_all(packed, "expert", 0, 0, axis_index_groups=order, tiled=True)
    ]
    far_down = pltpu.with_memory_space_constraint(w_down, pltpu.HBM)
    parts[0], w_down = fetch(True, far_down, parts[0], {1: 0})
    w_down = fetch(False, far_down, w_down, {1: 0})
    for s in range(1, n_parts):
        turn = [(i, (i + s) % n_parts) for i in range(n_parts)]
        parts.append(lax.ppermute(parts[0], "hidden", turn))
    products = 2 * rows * depth * units
    own, x_rows, grad_rows, scaled, d_gate, d_up, *others = pl.pallas_call(
        functools.partial(rows_kernel, n_parts),
        in_specs=[IN_VMEM] * n_parts + [IN_HBM] * 2 + [IN_VMEM],
        out_specs=[IN_VMEM] * (n_parts + 5),
        out_shape=[
            shape((peers * tok_dev, depth + LANES), jnp.float32),
            shape((rows, depth), half),
            shape((rows, depth), half),
            shape((rows, units), half),
            shape((rows, units), half),
            shape((rows, units), half),
        ]
        + [shape((peers, tok_dev, depth + LANES), half)] * (n_parts - 1),
        scratch_shapes=[
            pltpu.VMEM(w_gate.shape, half),
            pltpu.VMEM(w_up.shape, half),
            pltpu.SemaphoreType.DMA((2,)),
        ],
        compiler_params=pltpu.CompilerParams(vmem_limit_bytes=VMEM_ROWS),
        cost_estimate=pl.CostEstimate(
            flops=5 * products, bytes_accessed=6 * depth * units, transcendentals=rows * units
        ),
        name="rows",
    )(
        *parts,
        pltpu.with_memory_space_constraint(w_gate, pltpu.HBM),
        pltpu.with_memory_space_constraint(w_up, pltpu.HBM),
        w_down,
    )
    for s in range(1, n_parts):
        turn = [(i, (i - s) % n_parts) for i in range(n_parts)]
        others[s - 1] = lax.ppermute(others[s - 1], "hidden", turn)
    send = pl.pallas_call(
        join_kernel,
        in_specs=[IN_VMEM] * n_parts,
        out_specs=IN_VMEM,
        out_shape=shape((peers, tok_dev, depth + LANES), half),
        compiler_params=pltpu.CompilerParams(vmem_limit_bytes=VMEM_SMALL),
        name="join",
    )(own, *others)
    got = lax.all_to_all(send, "expert", 0, 0, axis_index_groups=order, tiled=True)
    bands = 2 * pl.cdiv(depth, BAND) + pl.cdiv(units, BAND) + 3
    grad_gate, grad_up, grad_down, ids, probs = pl.pallas_call(
        outer_kernel,
        in_specs=[ANYWHERE] + [IN_VMEM] * 5 + [IN_HBM] * 2,
        out_specs=[IN_HBM] * 3 + [IN_VMEM] * 2,
        out_shape=[
            shape((1, depth, units), jnp.float32),
            shape((1, depth, units), jnp.float32),
            shape((1, units, depth), jnp.float32),
            shape((tok_dev, LANES), jnp.int32),
            shape((tok_dev, LANES), jnp.float32),
        ],
        scratch_shapes=[
            pltpu.VMEM((depth, units), jnp.float32),
            pltpu.VMEM((depth, units), jnp.float32),
            pltpu.VMEM((units, depth), jnp.float32),
            pltpu.VMEM(expert_ids.shape, expert_ids.dtype),
            pltpu.VMEM(router_logits.shape, router_logits.dtype),
            pltpu.SemaphoreType.DMA((bands,)),
            pltpu.SemaphoreType.DMA((2,)),
        ],
        compiler_params=pltpu.CompilerParams(vmem_limit_bytes=VMEM_OUTER),
        cost_estimate=pl.CostEstimate(
            flops=3 * products, bytes_accessed=12 * depth * units, transcendentals=0
        ),
        name="outer",
    )(
        send,
        x_rows,
        grad_rows,
        scaled,
        d_gate,
        d_up,
        pltpu.with_memory_space_constraint(expert_ids, pltpu.HBM),
        pltpu.with_memory_space_constraint(router_logits, pltpu.HBM),
    )
    grad_in, grad_logits = pl.pallas_call(
        finish_kernel,
        in_specs=[IN_VMEM] * 3,
        out_specs=[IN_VMEM] * 2,
        out_shape=[
            shape((1, tok_dev, depth), jnp.float32),
            shape((1, tok_dev, TOP), jnp.float32),
        ],
        compiler_params=pltpu.CompilerParams(vmem_limit_bytes=VMEM_SMALL),
        name="finish",
    )(got, ids, probs)
    return grad_in, grad_logits, grad_gate, grad_up, grad_down


def on_device(tokens, grad_out, expert_ids, router_logits, w_gate, w_up, w_down):
    tok_dev, peers = tokens.shape[1], lax.axis_size("expert")
    most, there = 2 * tok_dev * TOP, tok_dev * peers
    whole_lanes = tokens.shape[2] % BAND == 0 and w_gate.shape[2] % LANES == 0
    plan = every_token if there <= most and 2 * peers <= LANES and whole_lanes else routed_rows
    return plan(tokens, grad_out, expert_ids, router_logits, w_gate, w_up, w_down)


def solution(mesh):
    in_specs = (
        P("hidden", "expert", None),
        P("hidden", "expert", None),
        P("hidden", "expert", None),
        P("hidden", "expert", None),
        P("expert", None, "hidden"),
        P("expert", None, "hidden"),
        P("expert", "hidden", None),
    )
    out_specs = (
        P("hidden", "expert", None),
        P("hidden", "expert", None),
        P("expert", None, "hidden"),
        P("expert", None, "hidden"),
        P("expert", "hidden", None),
    )
    return jax.shard_map(
        on_device, mesh=mesh, in_specs=in_specs, out_specs=out_specs, check_vma=False
    )
```

```python
import functools

import jax
import jax.numpy as jnp
from jax import lax
from jax.experimental import pallas as pl
from jax.experimental.pallas import tpu as pltpu
from jax.sharding import PartitionSpec as P

TOP = 8
LANES = 128
BAND = 512
DEPTH_AT_ONCE = 1024
VMEM_ROWS = 24 * 2**20
VMEM_OUTER = 24 * 2**20
VMEM_SMALL = 4 * 2**20
IN_VMEM = pl.BlockSpec(memory_space=pltpu.VMEM)
ANYWHERE = pl.BlockSpec(memory_space=pl.ANY)
IN_HBM = pl.BlockSpec(memory_space=pltpu.HBM)


def expert_core(x_rows, grad_rows, gate_col, gate_weight, up_weight, down_weight):
    pre_gate = jnp.dot(x_rows, gate_weight, preferred_element_type=jnp.float32)
    pre_up = jnp.dot(x_rows, up_weight, preferred_element_type=jnp.float32)
    back_grad = lax.dot_general(
        grad_rows, down_weight, (((1,), (1,)), ((), ())), preferred_element_type=jnp.float32
    )
    sigmoid_gate = jax.nn.sigmoid(pre_gate)
    silu_gate = pre_gate * sigmoid_gate
    active = silu_gate * pre_up
    gate_grad = jnp.sum(active * back_grad, axis=-1)
    weight = gate_col.astype(jnp.float32)
    scaled = (weight * active).astype(jnp.bfloat16)
    weighted_back = weight * back_grad
    d_gate_pre = (
        weighted_back * pre_up * sigmoid_gate * (1.0 + pre_gate * (1.0 - sigmoid_gate))
    ).astype(jnp.bfloat16)
    d_up_pre = (weighted_back * silu_gate).astype(jnp.bfloat16)
    sum_gate = lax.dot_general(
        x_rows, d_gate_pre, (((0,), (0,)), ((), ())), preferred_element_type=jnp.float32
    )
    sum_up = lax.dot_general(
        x_rows, d_up_pre, (((0,), (0,)), ((), ())), preferred_element_type=jnp.float32
    )
    sum_down = lax.dot_general(
        scaled, grad_rows, (((0,), (0,)), ((), ())), preferred_element_type=jnp.float32
    )
    return (gate_grad, d_gate_pre, d_up_pre, sum_gate, sum_up, sum_down)


def project_back(d_gate_pre, d_up_pre, gate_weight, up_weight):
    row_grad = lax.dot_general(
        d_gate_pre, gate_weight, (((1,), (1,)), ((), ())), preferred_element_type=jnp.float32
    )
    return row_grad + lax.dot_general(
        d_up_pre, up_weight, (((1,), (1,)), ((), ())), preferred_element_type=jnp.float32
    )


def routed_rows(tokens, grad_out, expert_ids, router_logits, w_gate, w_up, w_down):
    highest = lax.Precision.HIGHEST
    tok_dev = tokens.shape[1]
    peers = lax.axis_size("expert")
    mine = lax.axis_index("expert")
    row_cap = min(2 * tok_dev * TOP, tok_dev * peers)
    raised = jnp.exp(router_logits[0])
    gate_probs = raised / jnp.sum(raised, axis=-1, keepdims=True)
    gate_rows = gate_probs.astype(jnp.bfloat16)
    expert_range = jnp.arange(peers, dtype=jnp.int32)
    chosen = expert_ids[0][:, :, None] == expert_range[None, None, :]
    per_peer = jnp.sum(
        jnp.where(chosen, gate_rows.astype(jnp.float32)[:, :, None], jnp.float32(0.0)), axis=1
    )
    gate_table = per_peer.astype(jnp.bfloat16)
    got_x, got_grad, got_table = (
        lax.all_gather(tokens, "expert", axis=1, tiled=True),
        lax.all_gather(grad_out, "expert", axis=1, tiled=True),
        lax.all_gather(gate_table[None], "expert", axis=1, tiled=True),
    )
    all_x = got_x[0]
    all_grad = got_grad[0]
    column = jnp.sum(
        jnp.where(
            expert_range[None, :] == mine, got_table[0].astype(jnp.float32), jnp.float32(0.0)
        ),
        axis=-1,
    )
    picked = column > 0.0
    row_order = jnp.cumsum(picked.astype(jnp.int32)) - 1
    placing = (row_order[None, :] == jnp.arange(row_cap, dtype=jnp.int32)[:, None]) & picked[
        None, :
    ]
    placing_half = placing.astype(jnp.bfloat16)
    placing_full = placing.astype(jnp.float32)
    x_rows = jnp.dot(placing_half, all_x, preferred_element_type=jnp.float32).astype(jnp.bfloat16)
    grad_rows = jnp.dot(placing_half, all_grad, preferred_element_type=jnp.float32).astype(
        jnp.bfloat16
    )
    gate_col = jnp.dot(placing_full, column, precision=highest).astype(jnp.bfloat16)[:, None]
    gate_weight = w_gate[0]
    up_weight = w_up[0]
    down_weight = w_down[0]
    cycle_x, cycle_grad, cycle_gate = (
        lax.all_gather(x_rows, "hidden", axis=0, tiled=True),
        lax.all_gather(grad_rows, "hidden", axis=0, tiled=True),
        lax.all_gather(gate_col, "hidden", axis=0, tiled=True),
    )
    gate_part, gate_pre_all, up_pre_all, sum_gate, sum_up, sum_down = expert_core(
        cycle_x, cycle_grad, cycle_gate, gate_weight, up_weight, down_weight
    )
    row_part = project_back(gate_pre_all, up_pre_all, gate_weight, up_weight)
    own_rows, own_gate = (
        lax.psum_scatter(row_part, "hidden", scatter_dimension=0, tiled=True),
        lax.psum_scatter(gate_part, "hidden", scatter_dimension=0, tiled=True),
    )
    dense = lax.dot_general(placing_full, own_rows, (((0,), (0,)), ((), ())), precision=highest)
    token_gate = lax.dot_general(
        placing_full, own_gate, (((0,), (0,)), ((), ())), precision=highest
    )
    gate_out = jnp.where(expert_range[None, :] == mine, token_gate[:, None], jnp.float32(0.0))
    summed, gate_sums = (
        lax.psum_scatter(dense[None], "expert", scatter_dimension=1, tiled=True),
        lax.psum_scatter(gate_out[None], "expert", scatter_dimension=1, tiled=True),
    )
    gate_grad = jnp.sum(jnp.where(chosen, gate_sums[0][:, None, :], jnp.float32(0.0)), axis=-1)
    grad_logits = gate_probs * (gate_grad - jnp.sum(gate_probs * gate_grad, axis=-1, keepdims=True))
    return (summed, grad_logits[None], sum_gate[None], sum_up[None], sum_down[None])


def gate_probs_of(logits):
    raised = jnp.exp(logits)
    return raised / jnp.sum(raised, axis=-1, keepdims=True)


def pack_kernel(tokens_ref, grads_ref, ids_ref, logits_ref, out_ref):
    tok_dev, depth = tokens_ref.shape[1:]
    shares = gate_probs_of(logits_ref[0]).astype(jnp.bfloat16).astype(jnp.float32)
    ids = ids_ref[0]
    lane = lax.broadcasted_iota(jnp.int32, (tok_dev, LANES), 1)
    gates = jnp.zeros((tok_dev, LANES), jnp.float32)
    for k in range(TOP):
        gates = jnp.where(lane == ids[:, k : k + 1], shares[:, k : k + 1], gates)
    gates = gates.astype(jnp.bfloat16)
    tokens, grads = tokens_ref[0], grads_ref[0]
    for peer in range(out_ref.shape[0]):
        out_ref[peer, :, :depth] = tokens
        out_ref[peer, :, depth : 2 * depth] = grads
        out_ref[peer, :, 2 * depth :] = gates


def fetch_kernel(last, far_ref, *refs):
    here_ref, sem = refs[-2:]
    on_last = lax.axis_index("hidden") == lax.axis_size("hidden") - 1

    @pl.when(on_last if last else jnp.logical_not(on_last))
    def _():
        copy = pltpu.make_async_copy(far_ref, here_ref, sem)
        copy.start()
        copy.wait()


def fetch(last, array, held, aliases):
    spec = [IN_HBM, ANYWHERE if last else IN_VMEM]
    here = pltpu.VMEM(array.shape, array.dtype)
    out = pl.pallas_call(
        functools.partial(fetch_kernel, last),
        in_specs=spec,
        out_specs=[ANYWHERE, IN_VMEM] if last else IN_VMEM,
        out_shape=[jax.ShapeDtypeStruct(held.shape, held.dtype), here] if last else here,
        input_output_aliases=aliases,
        scratch_shapes=[pltpu.SemaphoreType.DMA],
        compiler_params=pltpu.CompilerParams(vmem_limit_bytes=VMEM_SMALL),
        cost_estimate=pl.CostEstimate(
            flops=0, bytes_accessed=2 * array.size * array.dtype.itemsize, transcendentals=0
        ),
        name="fetch",
    )(array, held)
    return out


def split_in_lanes(values):
    high = values.astype(jnp.bfloat16).astype(jnp.float32)
    return high + pltpu.roll(values - high, LANES // 2, 1)


def join_lanes(parts):
    lane = lax.broadcasted_iota(jnp.int32, parts.shape, 1)
    return jnp.where(lane < LANES // 2, parts + pltpu.roll(parts, LANES // 2, 1), 0.0)


def rows_kernel(n_parts, *refs):
    parts = refs[:n_parts]
    far_gate_ref, far_up_ref, w_down_ref = refs[n_parts : n_parts + 3]
    own_ref, x_ref, o_ref, scaled_ref, d_gate_ref, d_up_ref = refs[n_parts + 3 : n_parts + 9]
    other_refs = refs[n_parts + 9 : 2 * n_parts + 8]
    w_gate_ref, w_up_ref, sems = refs[2 * n_parts + 8 :]
    bring_gate = pltpu.make_async_copy(far_gate_ref, w_gate_ref, sems.at[0])
    bring_up = pltpu.make_async_copy(far_up_ref, w_up_ref, sems.at[1])
    bring_gate.start()
    peers, tok_dev, width = parts[0].shape
    depth = x_ref.shape[1]
    each = peers * tok_dev
    mine = lax.axis_index("expert")
    gates = []
    for s, part in enumerate(parts):
        rows = part[...].reshape(each, width)
        x_ref[s * each : (s + 1) * each, :] = rows[:, :depth]
        o_ref[s * each : (s + 1) * each, :] = rows[:, depth : 2 * depth]
        gates.append(rows[:, 2 * depth :].astype(jnp.float32))
    bring_up.start()
    gates = jnp.concatenate(gates, axis=0)
    own_lane = lax.broadcasted_iota(jnp.int32, gates.shape, 1) == mine
    weight = jnp.sum(jnp.where(own_lane, gates, 0.0), axis=-1, keepdims=True)
    x_rows, grad_rows = x_ref[...], o_ref[...]
    across = (((1,), (1,)), ((), ()))
    back_grad = lax.dot_general(
        grad_rows, w_down_ref[0], across, preferred_element_type=jnp.float32
    )
    bring_gate.wait()
    pre_gate = jnp.dot(x_rows, w_gate_ref[0], preferred_element_type=jnp.float32)
    bring_up.wait()
    pre_up = jnp.dot(x_rows, w_up_ref[0], preferred_element_type=jnp.float32)
    sigmoid_gate = 1.0 / (1.0 + jnp.exp(-pre_gate))
    silu_gate = pre_gate * sigmoid_gate
    active = silu_gate * pre_up
    gate_part = jnp.sum(active * back_grad, axis=-1, keepdims=True)
    weighted_back = weight * back_grad
    d_gate = (
        weighted_back * pre_up * sigmoid_gate * (1.0 + pre_gate * (1.0 - sigmoid_gate))
    ).astype(jnp.bfloat16)
    d_up = (weighted_back * silu_gate).astype(jnp.bfloat16)
    scaled_ref[...] = (weight * active).astype(jnp.bfloat16)
    d_gate_ref[...] = d_gate
    d_up_ref[...] = d_up
    def put(value, start):
        cols = slice(start, start + value.shape[1])
        own_ref[:, cols] = value[:each]
        for s, other in enumerate(other_refs, 1):
            block = value[s * each : (s + 1) * each].astype(jnp.bfloat16)
            other[:, :, cols] = block.reshape(peers, tok_dev, value.shape[1])

    put(split_in_lanes(jnp.where(own_lane, gate_part, 0.0)), depth)
    for start in range(0, depth, DEPTH_AT_ONCE):
        at = slice(start, min(start + DEPTH_AT_ONCE, depth))
        row_grad = lax.dot_general(
            w_gate_ref[0, at, :], d_gate, across, preferred_element_type=jnp.float32
        ) + lax.dot_general(
            w_up_ref[0, at, :], d_up, across, preferred_element_type=jnp.float32
        )
        put(row_grad.T, start)


def join_kernel(own_ref, *refs):
    send_ref = refs[-1]
    peers, tok_dev, width = send_ref.shape
    depth = width - LANES
    total, gates = own_ref[:, :depth], join_lanes(own_ref[:, depth:])
    for other in refs[:-1]:
        rows = other[...].reshape(peers * tok_dev, width).astype(jnp.float32)
        total, gates = total + rows[:, :depth], gates + join_lanes(rows[:, depth:])
    for value, cols in (
        (total, slice(0, depth)),
        (split_in_lanes(gates), slice(depth, width)),
    ):
        send_ref[:, :, cols] = value.astype(jnp.bfloat16).reshape(peers, tok_dev, value.shape[1])


def outer_kernel(
    after_ref,
    x_ref,
    o_ref,
    scaled_ref,
    d_gate_ref,
    d_up_ref,
    ids_ref,
    logits_ref,
    *outs_and_scratch,
):
    gate_ref, up_ref, down_ref, ids_out, probs_out = outs_and_scratch[:5]
    *held, ids_here, logits_here, sems, router_sems = outs_and_scratch[5:]
    router = [
        pltpu.make_async_copy(ids_ref, ids_here, router_sems.at[0]),
        pltpu.make_async_copy(logits_ref, logits_here, router_sems.at[1]),
    ]
    for copy in router:
        copy.start()
    over_rows = (((0,), (0,)), ((), ()))
    work = (
        (x_ref, d_gate_ref, gate_ref, held[0]),
        (x_ref, d_up_ref, up_ref, held[1]),
        (scaled_ref, o_ref, down_ref, held[2]),
    )
    copies = []
    for left, right, out, here in work:
        end = left.shape[1]
        edges = sorted({0, min(LANES, end), *range(BAND, end, BAND), end})
        for band in (slice(*pair) for pair in zip(edges, edges[1:])):
            here[band, :] = lax.dot_general(
                left[:, band], right[...], over_rows, preferred_element_type=jnp.float32
            )
            copy = pltpu.make_async_copy(
                here.at[band], out.at[0, band], sems.at[len(copies)]
            )
            copy.start()
            copies.append(copy)
    for copy in router:
        copy.wait()
    ids_out[...] = jnp.zeros_like(ids_out)
    ids_out[:, :TOP] = ids_here[0]
    probs_out[...] = jnp.zeros_like(probs_out)
    probs_out[:, :TOP] = gate_probs_of(logits_here[0])
    for copy in copies:
        copy.wait()


def finish_kernel(got_ref, ids_ref, probs_ref, grad_in_ref, grad_logits_ref, held_ref, sem):
    depth = grad_in_ref.shape[-1]
    total = got_ref[0].astype(jnp.float32)
    for block in range(1, got_ref.shape[0]):
        total = total + got_ref[block].astype(jnp.float32)
    held_ref[0] = total[:, :depth]
    copy = pltpu.make_async_copy(held_ref, grad_in_ref, sem)
    copy.start()
    by_expert = total[:, depth:]
    probs, ids = probs_ref[...], ids_ref[...]
    gate_grad = jnp.take_along_axis(by_expert, ids, axis=1) + jnp.take_along_axis(
        by_expert, ids + LANES // 2, axis=1
    )
    mean = jnp.sum(probs * gate_grad, axis=-1, keepdims=True)
    grad_logits_ref[0] = (probs * (gate_grad - mean))[:, :TOP]
    copy.wait()


def every_token(tokens, grad_out, expert_ids, router_logits, w_gate, w_up, w_down):
    peers, n_parts = lax.axis_size("expert"), lax.axis_size("hidden")
    tok_dev, depth = tokens.shape[1:]
    units = w_gate.shape[2]
    rows = n_parts * peers * tok_dev
    half = jnp.bfloat16
    shape = jax.ShapeDtypeStruct
    packed = pl.pallas_call(
        pack_kernel,
        in_specs=[IN_VMEM] * 4,
        out_specs=IN_VMEM,
        out_shape=pltpu.VMEM((peers, tok_dev, 2 * depth + LANES), half),
        name="pack",
    )(tokens, grad_out, expert_ids, router_logits)
    order = [[(peer + peers // 2) % peers for peer in range(peers)]]
    parts = [
        lax.all_to_all(packed, "expert", 0, 0, axis_index_groups=order, tiled=True)
    ]
    far_down = pltpu.with_memory_space_constraint(w_down, pltpu.HBM)
    parts[0], w_down = fetch(True, far_down, parts[0], {1: 0})
    w_down = fetch(False, far_down, w_down, {1: 0})
    for s in range(1, n_parts):
        turn = [(i, (i + s) % n_parts) for i in range(n_parts)]
        parts.append(lax.ppermute(parts[0], "hidden", turn))
    products = 2 * rows * depth * units
    own, x_rows, grad_rows, scaled, d_gate, d_up, *others = pl.pallas_call(
        functools.partial(rows_kernel, n_parts),
        in_specs=[IN_VMEM] * n_parts + [IN_HBM] * 2 + [IN_VMEM],
        out_specs=[IN_VMEM] * (n_parts + 5),
        out_shape=[
            shape((peers * tok_dev, depth + LANES), jnp.float32),
            shape((rows, depth), half),
            shape((rows, depth), half),
            shape((rows, units), half),
            shape((rows, units), half),
            shape((rows, units), half),
        ]
        + [shape((peers, tok_dev, depth + LANES), half)] * (n_parts - 1),
        scratch_shapes=[
            pltpu.VMEM(w_gate.shape, half),
            pltpu.VMEM(w_up.shape, half),
            pltpu.SemaphoreType.DMA((2,)),
        ],
        compiler_params=pltpu.CompilerParams(vmem_limit_bytes=VMEM_ROWS),
        cost_estimate=pl.CostEstimate(
            flops=5 * products, bytes_accessed=6 * depth * units, transcendentals=rows * units
        ),
        name="rows",
    )(
        *parts,
        pltpu.with_memory_space_constraint(w_gate, pltpu.HBM),
        pltpu.with_memory_space_constraint(w_up, pltpu.HBM),
        w_down,
    )
    for s in range(1, n_parts):
        turn = [(i, (i - s) % n_parts) for i in range(n_parts)]
        others[s - 1] = lax.ppermute(others[s - 1], "hidden", turn)
    send = pl.pallas_call(
        join_kernel,
        in_specs=[IN_VMEM] * n_parts,
        out_specs=IN_VMEM,
        out_shape=shape((peers, tok_dev, depth + LANES), half),
        compiler_params=pltpu.CompilerParams(vmem_limit_bytes=VMEM_SMALL),
        name="join",
    )(own, *others)
    got = lax.all_to_all(send, "expert", 0, 0, axis_index_groups=order, tiled=True)
    bands = 2 * pl.cdiv(depth, BAND) + pl.cdiv(units, BAND) + 3
    grad_gate, grad_up, grad_down, ids, probs = pl.pallas_call(
        outer_kernel,
        in_specs=[ANYWHERE] + [IN_VMEM] * 5 + [IN_HBM] * 2,
        out_specs=[IN_HBM] * 3 + [IN_VMEM] * 2,
        out_shape=[
            shape((1, depth, units), jnp.float32),
            shape((1, depth, units), jnp.float32),
            shape((1, units, depth), jnp.float32),
            shape((tok_dev, LANES), jnp.int32),
            shape((tok_dev, LANES), jnp.float32),
        ],
        scratch_shapes=[
            pltpu.VMEM((depth, units), jnp.float32),
            pltpu.VMEM((depth, units), jnp.float32),
            pltpu.VMEM((units, depth), jnp.float32),
            pltpu.VMEM(expert_ids.shape, expert_ids.dtype),
            pltpu.VMEM(router_logits.shape, router_logits.dtype),
            pltpu.SemaphoreType.DMA((bands,)),
            pltpu.SemaphoreType.DMA((2,)),
        ],
        compiler_params=pltpu.CompilerParams(vmem_limit_bytes=VMEM_OUTER),
        cost_estimate=pl.CostEstimate(
            flops=3 * products, bytes_accessed=12 * depth * units, transcendentals=0
        ),
        name="outer",
    )(
        send,
        x_rows,
        grad_rows,
        scaled,
        d_gate,
        d_up,
        pltpu.with_memory_space_constraint(expert_ids, pltpu.HBM),
        pltpu.with_memory_space_constraint(router_logits, pltpu.HBM),
    )
    grad_in, grad_logits = pl.pallas_call(
        finish_kernel,
        in_specs=[IN_VMEM] * 3,
        out_specs=[IN_HBM, IN_VMEM],
        scratch_shapes=[
            pltpu.VMEM((1, tok_dev, depth), jnp.float32),
            pltpu.SemaphoreType.DMA,
        ],
        out_shape=[
            shape((1, tok_dev, depth), jnp.float32),
            shape((1, tok_dev, TOP), jnp.float32),
        ],
        compiler_params=pltpu.CompilerParams(vmem_limit_bytes=VMEM_SMALL),
        name="finish",
    )(got, ids, probs)
    return grad_in, grad_logits, grad_gate, grad_up, grad_down


def on_device(tokens, grad_out, expert_ids, router_logits, w_gate, w_up, w_down):
    tok_dev, peers = tokens.shape[1], lax.axis_size("expert")
    most, there = 2 * tok_dev * TOP, tok_dev * peers
    whole_lanes = tokens.shape[2] % BAND == 0 and w_gate.shape[2] % LANES == 0
    plan = every_token if there <= most and 2 * peers <= LANES and whole_lanes else routed_rows
    return plan(tokens, grad_out, expert_ids, router_logits, w_gate, w_up, w_down)


def solution(mesh):
    in_specs = (
        P("hidden", "expert", None),
        P("hidden", "expert", None),
        P("hidden", "expert", None),
        P("hidden", "expert", None),
        P("expert", None, "hidden"),
        P("expert", None, "hidden"),
        P("expert", "hidden", None),
    )
    out_specs = (
        P("hidden", "expert", None),
        P("hidden", "expert", None),
        P("expert", None, "hidden"),
        P("expert", None, "hidden"),
        P("expert", "hidden", None),
    )
    return jax.shard_map(
        on_device, mesh=mesh, in_specs=in_specs, out_specs=out_specs, check_vma=False
    )
```
